256 devices in a mesh: kv: 8 (over x, y_lo), ctx: 32 (over y_hi, z, core).
Axes of the slice: x: 4, y: 4 (y_hi: 2, y_lo: 2; y = y_hi * 2 + y_lo), z: 8, core: 2. Of those that a mesh axis runs over, the one named last changes fastest.
Arguments:
- hidden: bfloat16 [16384, 4096], P('ctx', 'kv'), may hold values from -16 to 16
- w_query: bfloat16 [4096, 4096], P(None, 'kv'), may hold values from -0.09375 to 0.09375
- w_key: bfloat16 [4096, 1024], P(None, 'kv'), may hold values from -0.09375 to 0.09375
- w_value: bfloat16 [4096, 1024], P(None, 'kv'), may hold values from -0.09375 to 0.09375
- keep_rows: int32 [2048], P('ctx'), may hold values from 0 to 511, as said below
- keep_count: int32 [32], replicated, may hold values from 32 to 64, as said below
Outputs:
- context: bfloat16 [16384, 4096], P('ctx', 'kv')
The draws below stay inside these ranges and needn't reach their ends.
Inputs may be any that keep to these rules, and one draw needn't show every extreme that they name: `keep_rows`: the 64 slots of each block name distinct rows of that block in rising order; row 0 and row 511 of every block are always named. `keep_count`: some block has a count of 64 and some block a count of exactly 32.
All inputs are finite; a program needn't handle non-finite values.
Results may differ from the reference program's by a relative error of at most 0.015.
The reference program's roundings to bfloat16 on the way (of `query`, `key`, `value` and `weights`) count: a program that leaves them out, or rounds other values in their place, can miss the bound.
Values may be sent and summed in bfloat16 or wider, within the bound.
A program may use at most 64 MiB of HBM per device.

```python
import math
import jax
import jax.numpy as jnp
from jax import lax

D = 4096
HD = 128
TOK_DEV = 512
KEEP = 64
KV_HEADS = 8
QHEADS = 32
TOKENS = 16384
N_CTX = 32


def draw_hidden(key, part):
    key = jax.random.fold_in(key, 11)
    first = jax.random.fold_in(key, 0)
    field = jnp.clip(jax.random.normal(first, (TOKENS, D), jnp.float32), -6.0, 6.0)
    return field.astype(jnp.bfloat16)


def draw_keep_rows(key, part):
    key = jax.random.fold_in(key, 23)
    ranks = jax.random.randint(key, (N_CTX, TOK_DEV), 0, 1 << 20)
    places = jnp.arange(TOK_DEV, dtype=jnp.int32)[None, :]
    ranks = ranks * TOK_DEV + places
    ends = (places == 0) | (places == TOK_DEV - 1)
    ranks = jnp.where(ends, (1 << 30) + places, ranks)
    picked = lax.top_k(ranks, KEEP)[1]
    picked = jnp.sort(picked, axis=1)
    return picked.reshape(-1).astype(jnp.int32)


def draw_keep_count(key, part):
    key = jax.random.fold_in(key, 37)
    first, second = jax.random.split(key)
    counts = jax.random.randint(first, (N_CTX,), KEEP // 2, KEEP + 1)
    chosen = jax.random.randint(second, (), 0, N_CTX)
    places = jnp.arange(N_CTX, dtype=jnp.int32)
    counts = jnp.where(places == chosen, KEEP, counts)
    counts = jnp.where(places == (chosen + 1) % N_CTX, KEEP // 2, counts)
    return counts.astype(jnp.int32)


def levels(own_key, dims, shards, smallest, top_value):
    loudness, own = 1.0, jax.random.fold_in(own_key, 6)
    for position, shards_of in shards:
        draws = jnp.exp(jax.random.uniform(jax.random.fold_in(own, position), (shards_of,), jnp.float32, smallest / len(shards), top_value / len(shards)))
        loudness = loudness * jnp.repeat(draws, dims[position] // shards_of).reshape([-1 if axis == position else 1 for axis in range(len(dims))])
    return loudness


def bell_draw(own_key, extent, spread, most, cuts=(), kind=jnp.bfloat16):
    level = levels(own_key, extent, cuts, -0.22, 0.18) if cuts else 1.0
    entries = jax.random.normal(own_key, extent, jnp.float32) * spread * level
    return jnp.minimum(jnp.maximum(entries, -most), most).astype(kind)


def setup_inputs(seed: int = 0) -> dict:
    splits = jax.random.split(jax.random.key(seed), 7)
    hidden = draw_hidden(jax.random.fold_in(splits[6], 71), 0)
    w_query = bell_draw(splits[1], (D, QHEADS * HD), D ** -0.5, 0.09375, ((1, 8),))
    w_key = bell_draw(splits[2], (D, KV_HEADS * HD), D ** -0.5, 0.09375, ((1, 8),))
    w_value = bell_draw(splits[3], (D, KV_HEADS * HD), D ** -0.5, 0.09375, ((1, 8),))
    keep_rows = draw_keep_rows(jax.random.fold_in(splits[6], 71), 0)
    keep_count = draw_keep_count(jax.random.fold_in(splits[6], 71), 0)
    return dict(hidden=hidden, w_query=w_query, w_key=w_key, w_value=w_value, keep_rows=keep_rows, keep_count=keep_count)


def rotate(field, places):
    half = field.shape[-1] // 2
    freq = 500000.0 ** (-(jnp.arange(half, dtype=jnp.float32) * 2.0 / field.shape[-1]))
    angles = places.astype(jnp.float32)[:, None] * freq[None, :]
    cosine = jnp.cos(angles)[:, None, :]
    sine = jnp.sin(angles)[:, None, :]
    first = field[..., :half]
    second = field[..., half:]
    return jnp.concatenate([first * cosine - second * sine, second * cosine + first * sine], axis=-1)

def reference(hidden, w_query, w_key, w_value, keep_rows, keep_count):
    total = hidden.shape[0]
    places = jnp.arange(total, dtype=jnp.int32)
    query = rotate(jnp.dot(hidden, w_query, preferred_element_type=jnp.float32).reshape(total, QHEADS, HD), places).astype(jnp.bfloat16)
    key = rotate(jnp.dot(hidden, w_key, preferred_element_type=jnp.float32).reshape(total, KV_HEADS, HD), places).astype(jnp.bfloat16)
    value = jnp.dot(hidden, w_value, preferred_element_type=jnp.float32).reshape(total, KV_HEADS, HD).astype(jnp.bfloat16)
    slots = N_CTX * KEEP
    slot_host = jnp.arange(slots, dtype=jnp.int32) // KEEP
    slot_pos = jnp.arange(slots, dtype=jnp.int32) % KEEP
    chosen = (slot_host * TOK_DEV + keep_rows).astype(jnp.int32)
    passed_key = key[chosen]
    passed_value = value[chosen]
    live_base = (slot_pos < keep_count[slot_host]) & (slot_host >= 1)
    local = jnp.arange(TOK_DEV, dtype=jnp.int32)
    causal = local[None, :] <= local[:, None]
    group = QHEADS // KV_HEADS

    def one_block(block):
        start = (block * TOK_DEV).astype(jnp.int32)
        block_q = lax.dynamic_slice_in_dim(query, start, TOK_DEV, 0)
        block_k = lax.dynamic_slice_in_dim(key, start, TOK_DEV, 0)
        block_v = lax.dynamic_slice_in_dim(value, start, TOK_DEV, 0)
        keys = jnp.concatenate([key[:TOK_DEV], passed_key, block_k], axis=0)
        values = jnp.concatenate([value[:TOK_DEV], passed_value, block_v], axis=0)
        live = live_base & (slot_host < block)
        mask = jnp.concatenate([jnp.broadcast_to(block > 0, (TOK_DEV, TOK_DEV)), jnp.broadcast_to(live[None, :], (TOK_DEV, slots)), causal], axis=1)
        grouped = block_q.reshape(TOK_DEV, KV_HEADS, group, HD).astype(jnp.float32)
        scores = jnp.einsum('tkgd,skd->kgts', grouped, keys.astype(jnp.float32)) / math.sqrt(HD)
        scores = jnp.where(mask[None, None], scores, -jnp.inf)
        top = lax.optimization_barrier(jnp.max(scores, axis=-1, keepdims=True))
        expo = jnp.exp(scores - top)
        weights = (expo / lax.optimization_barrier(jnp.sum(expo, axis=-1, keepdims=True))).astype(jnp.bfloat16)
        out = jnp.einsum('kgts,skd->tkgd', weights.astype(jnp.float32), values.astype(jnp.float32))
        return out.reshape(TOK_DEV, QHEADS * HD).astype(jnp.bfloat16)
    blocks = lax.map(one_block, jnp.arange(N_CTX, dtype=jnp.int32))
    return blocks.reshape(total, QHEADS * HD)
```

```python
import functools
import math

import jax
import jax.numpy as jnp
import numpy as np
from jax import lax
from jax.experimental import pallas as pl
from jax.experimental.pallas import tpu as pltpu
from jax.sharding import PartitionSpec as P

HD = 128
MESH = pl.DeviceIdType.MESH
BF = jnp.bfloat16
F32 = jnp.float32
SCALE = math.log2(math.e) / math.sqrt(HD)
TILE = 512


class Wire:
    def __init__(self, send, recv):
        self.send, self.recv, self.copies = send, recv, []

    def go(self, src, dst, device):
        n = len(self.copies)
        copy = pltpu.make_async_remote_copy(
            src_ref=src,
            dst_ref=dst,
            send_sem=self.send.at[n],
            recv_sem=self.recv.at[n],
            device_id=device,
            device_id_type=MESH,
        )
        copy.start()
        self.copies.append(copy)
        return copy


def up16(n):
    return (n + 15) // 16 * 16


class Gather:
    def __init__(self, wire, buf, base, rows, cut, kv_at, source=None):
        self.wire, self.buf, self.base, self.rows, self.cut, self.at = wire, buf, base, rows, cut, kv_at
        me = kv_at(0, 0)
        self.source = buf.at[me, pl.ds(base, rows)] if source is None else source

    def part(self, dx, dy, lo, hi):
        return self.buf.at[self.at(dx, dy), pl.ds(self.base + lo, hi - lo)]

    def fwd(self, part, dx, dy):
        return self.wire.go(part, part, {"kv": self.at(dx, dy)})

    def own(self):
        dst = self.part(0, 0, 0, self.rows)
        self.first = [
            self.wire.go(self.source, dst, {"kv": self.at(dx, dy)}) for dx, dy in ((1, 0), (3, 0), (0, 1))
        ]

    def second(self):
        n, cut, half = self.rows, self.cut, up16(self.rows // 2)
        from_left, from_right, from_y = self.first
        from_y.wait_recv()
        part = self.part(0, 1, cut, n)
        self.b_left = self.fwd(part, 1, 0)
        self.b_right = self.fwd(part, 3, 0)
        from_left.wait_recv()
        self.far0 = self.fwd(self.part(3, 0, 0, half), 1, 0)
        self.y_left = self.fwd(self.part(3, 0, 0, cut), 0, 1)
        from_right.wait_recv()
        self.far1 = self.fwd(self.part(1, 0, half, n), 3, 0)
        self.y_right = self.fwd(self.part(1, 0, 0, cut), 0, 1)

    def third(self):
        n, cut = self.rows, self.cut
        mid = cut + up16((n - cut) // 2)
        self.b_left.wait_recv()
        self.bfar0 = self.fwd(self.part(3, 1, cut, mid), 1, 0)
        self.b_right.wait_recv()
        self.bfar1 = self.fwd(self.part(1, 1, mid, n), 3, 0)
        self.far0.wait_recv()
        self.far1.wait_recv()
        self.y_far = self.fwd(self.part(2, 0, 0, cut), 0, 1)

    def finish(self):
        for copy in (self.y_left, self.y_right, self.bfar0, self.bfar1, self.y_far):
            copy.wait_recv()


def rope(field, cosine, sine):
    return field * cosine + pltpu.roll(field, HD // 2, 1) * sine


def tables(places, freq, sign):
    angles = places * freq
    return jnp.cos(angles), jnp.sin(angles) * sign


def kernel(
    sizes,
    hidden, w_query, w_key, w_value, keep_rows, keep_count, freq,
    out,
    H, RH, W, G, KR, VR, KL, VL, Q, S, cos_t, sin_t, freq_v, out_v,
    send, recv, a_send, a_recv, l_sem,
):
    rows, keep, share, groups, n_ctx, nz = sizes
    chunk = 128
    n_chunks = rows // chunk
    slots = keep + share
    kv = lax.axis_index("kv")
    ctx = lax.axis_index("ctx")
    kx, ky = kv // 2, kv % 2
    yh, z, core = ctx // (2 * nz), (ctx // 2) % nz, ctx % 2

    def kv_at(dx, dy):
        return ((kx + dx) % 4) * 2 + (ky + dy) % 2

    def ctx_at(dy, dz, dc):
        return ((yh + dy) % 2) * (2 * nz) + ((z + dz) % nz) * 2 + (core + dc) % 2

    local = []

    def fetch(src, dst):
        copy = pltpu.make_async_copy(src, dst, l_sem.at[len(local)])
        copy.start()
        local.append(copy)
        return copy

    own_here = fetch(hidden, H.at[kv])
    got_freq = fetch(freq, freq_v)
    got_w = [
        fetch(w_key, W.at[:, pl.ds(groups * HD, HD)]),
        fetch(w_value, W.at[:, pl.ds((groups + 1) * HD, HD)]),
        fetch(w_query, W.at[:, pl.ds(0, groups * HD)]),
    ]

    barrier = pltpu.get_barrier_semaphore()
    kv_near = ((1, 0), (3, 0), (0, 1))
    ctx_near = ((1, 0, 0), (0, 1, 0), (0, nz - 1, 0), (0, 2, 0), (0, nz - 2, 0), (0, 0, 1))
    for step in kv_near:
        pl.semaphore_signal(barrier, inc=1, device_id={"kv": kv_at(*step)}, device_id_type=MESH)
    for step in ctx_near:
        pl.semaphore_signal(barrier, inc=1, device_id={"ctx": ctx_at(*step)}, device_id_type=MESH)

    @pl.when(ctx != 0)
    def _():
        pl.semaphore_signal(barrier, inc=1, device_id={"ctx": 0}, device_id_type=MESH)

    near = len(kv_near) + len(ctx_near)
    pl.semaphore_wait(barrier, jnp.where(ctx == 0, near + n_ctx - 1, near))

    wire = Wire(send, recv)
    anchor_slot = RH.at[kv, pl.ds(keep, share)]

    def anchor_copy(c):
        return pltpu.make_async_remote_copy(
            src_ref=hidden.at[pl.ds(c * share, share)],
            dst_ref=anchor_slot,
            send_sem=a_send.at[c],
            recv_sem=a_recv,
            device_id={"ctx": c},
            device_id_type=MESH,
        )

    @pl.when(ctx == 0)
    def _():
        def body(c, carry):
            anchor_copy(c).start()
            return carry

        lax.fori_loop(1, n_ctx, body, 0)
        mine = pltpu.make_async_copy(hidden.at[pl.ds(0, share)], anchor_slot, a_recv)
        mine.start()

    parts = [
        Gather(wire, H, r * chunk, chunk, 64, kv_at, hidden.at[pl.ds(r * chunk, chunk)]) for r in range(n_chunks)
    ]
    extra = Gather(wire, RH, 0, slots, 32, kv_at)
    parts[0].own()

    place_of = lax.broadcasted_iota(jnp.int32, (keep, HD), 0)
    picked = jnp.zeros((keep, HD), jnp.int32)
    for j in range(keep):
        picked = jnp.where(place_of == j, keep_rows[j], picked)
    lanes = lax.broadcasted_iota(jnp.int32, (keep, HD), 1)
    one_hot = jnp.concatenate(
        [(lanes + k * HD == picked).astype(F32).astype(BF) for k in range(rows // HD)], axis=1
    )
    own_here.wait()
    RH[kv, 0:keep] = jnp.dot(one_hot, H[kv], preferred_element_type=F32).astype(BF)
    anchor_copy(0).wait_recv()
    extra.own()
    parts[1].own()

    got_freq.wait()
    freq_row = freq_v[0:1, :]
    lane = lax.broadcasted_iota(jnp.int32, (1, HD), 1)
    sign = jnp.where(lane < HD // 2, -1.0, 1.0)

    def table_of(i, carry):
        at = pl.ds(pl.multiple_of(i * 64, 64), 64)
        places = (ctx * rows + i * 64 + lax.broadcasted_iota(jnp.int32, (64, HD), 0)).astype(F32)
        cos_t[at, :], sin_t[at, :] = tables(places, freq_row, sign)
        return carry

    parts[0].second()
    extra.second()
    lax.fori_loop(0, rows // 64, table_of, 0)
    extra_places = jnp.concatenate(
        [
            (ctx * rows + picked).astype(F32),
            (ctx * share + lax.broadcasted_iota(jnp.int32, (share, HD), 0)).astype(F32),
        ],
        axis=0,
    )
    extra_cos, extra_sin = tables(extra_places, freq_row, sign)
    parts[0].third()
    extra.third()
    parts[2].own()
    for copy in got_w:
        copy.wait()
    depth = hidden.shape[1]
    n_src = H.shape[0]
    extra.finish()
    kv_cols = slice(groups * HD, (groups + 2) * HD)
    raw = jnp.zeros((slots, 2 * HD), F32)
    for s in range(n_src):
        raw += jnp.dot(RH[s], W[s * depth : (s + 1) * depth, kv_cols], preferred_element_type=F32)
    G[core, z, yh, :, 0:HD] = rope(raw[:, :HD], extra_cos, extra_sin).astype(BF)
    G[core, z, yh, :, HD:] = raw[:, HD:].astype(BF)

    def hop(part, step):
        return wire.go(part, part, {"ctx": ctx_at(*step)})

    def at_z(dz):
        return G.at[core, (z + dz) % nz]

    across = hop(G.at[core, z, yh], (1, 0, 0))
    parts[1].second()

    def project(r):
        part = slice(r * chunk, (r + 1) * chunk)
        raw = jnp.zeros((chunk, (groups + 2) * HD), F32)
        for s in range(n_src):
            raw += jnp.dot(H[s, part], W[s * depth : (s + 1) * depth], preferred_element_type=F32)
        cosine, sine = cos_t[part], sin_t[part]
        for g in range(groups):
            Q[r, g * chunk : (g + 1) * chunk] = rope(raw[:, g * HD : (g + 1) * HD], cosine, sine).astype(BF)
        KL[part] = rope(raw[:, groups * HD : (groups + 1) * HD], cosine, sine).astype(BF)
        VL[part, 0:HD] = raw[:, (groups + 1) * HD :].astype(BF)
        VL[part, HD:] = jnp.ones((chunk, HD), BF)

    across.wait_recv()
    pair = at_z(0)
    near_z = {dz: hop(pair, (0, dz, 0)) for dz in (1, nz - 1, 2, nz - 2)}
    to_core = [hop(pair, (0, 0, 1))]
    parts[0].finish()
    project(0)
    parts[1].third()
    parts[3].own()

    far = []
    for dz, half in ((2, 0), (nz - 2, 1)):
        near_z[dz].wait_recv()
        got = at_z(nz - dz)
        one = 1 if dz == 2 else nz - 1
        far.append((hop(got, (0, one, 0)), one))
        far.append((hop(G.at[core, (z + nz - dz) % nz, half], (0, dz, 0)), half))
        to_core.append(hop(got, (0, 0, 1)))
    for dz in (1, nz - 1):
        near_z[dz].wait_recv()
        to_core.append(hop(at_z(nz - dz), (0, 0, 1)))
    parts[2].second()
    parts[1].finish()
    project(1)
    for i, dz in ((0, 3), (2, nz - 3)):
        far[i][0].wait_recv()
        to_core.append(hop(at_z(nz - dz), (0, 0, 1)))
    for i, half in ((1, 0), (3, 1)):
        far[i][0].wait_recv()
        to_core.append(hop(G.at[core, (z + nz // 2) % nz, half], (0, 0, 1)))
    parts[2].third()
    parts[3].second()
    for copy in to_core:
        copy.wait_recv()

    first_key = KL[0:16].astype(F32)[0:1]
    row_of = lax.broadcasted_iota(jnp.int32, (slots, HD), 0)

    def ready(i, carry):
        c = (i % 2) * (2 * nz) + ((i // 2) % nz) * 2 + i // (2 * nz)
        limit = jnp.where((c >= 1) & (c < ctx), keep_count[c], 0)
        limit_a = jnp.where(ctx >= 1, slots, 0)
        live = row_of < jnp.where(row_of < keep, limit, limit_a)
        block = G[i // (2 * nz), (i // 2) % nz, i % 2].astype(F32)
        at = pl.ds(pl.multiple_of(i * slots, 16), slots)
        KR[at, :] = jnp.where(live, block[:, :HD], first_key).astype(BF)
        VR[at, 0:HD] = jnp.where(live, block[:, HD:], 0.0).astype(BF)
        VR[at, HD:] = live.astype(F32).astype(BF)
        return carry

    lax.fori_loop(0, n_ctx, ready, 0)

    many = groups * chunk
    n_far = n_ctx * slots
    contract = (((1,), (1,)), ((), ()))
    in_chunk = lax.broadcasted_iota(jnp.int32, (many, chunk), 0) % chunk
    causal = lax.broadcasted_iota(jnp.int32, (many, chunk), 1) <= in_chunk

    def lane_max(s):
        top = s[:, :HD]
        for k in range(1, s.shape[1] // HD):
            top = jnp.maximum(top, s[:, k * HD : (k + 1) * HD])
        return top

    def attend(r):
        q = Q[r]
        near_keys = (r + 1) * chunk

        def scores(keys):
            return lax.dot_general(q, keys, contract, preferred_element_type=F32) * SCALE

        s = scores(KL[0:near_keys])
        diagonal = jnp.where(causal, s[:, r * chunk :], -jnp.inf)
        top = diagonal
        if r:
            s = s[:, : r * chunk]
            S[:, n_far : n_far + r * chunk] = s
            top = jnp.maximum(top, lane_max(s))
        S[:, n_far + r * chunk : n_far + near_keys] = diagonal

        def first(i, top):
            at = pl.ds(pl.multiple_of(i * TILE, TILE), TILE)
            s = scores(KR[at, :])
            S[:, at] = s
            return jnp.maximum(top, lane_max(s))

        top = lax.fori_loop(0, n_far // TILE, first, top)
        top = jnp.max(top, axis=1, keepdims=True)

        def weigh(s, values):
            return jnp.dot(jnp.exp2(s - top).astype(BF), values, preferred_element_type=F32)

        total = weigh(S[:, n_far : n_far + near_keys], VL[0:near_keys])

        def second(i, total):
            at = pl.ds(pl.multiple_of(i * TILE, TILE), TILE)
            return total + weigh(S[:, at], VR[at, :])

        total = lax.fori_loop(0, n_far // TILE, second, total)
        result = (total[:, :HD] / total[:, HD:]).astype(BF)
        part = slice(r * chunk, (r + 1) * chunk)
        for g in range(groups):
            out_v[part, g * HD : (g + 1) * HD] = result[g * chunk : (g + 1) * chunk]
        return fetch(out_v.at[part], out.at[part])

    parts[2].finish()
    project(2)
    written = [attend(0)]
    parts[3].third()
    written += [attend(1), attend(2)]
    parts[3].finish()
    project(3)
    written.append(attend(3))
    for copy in written:
        copy.wait()
    for copy in wire.copies:
        copy.wait_send()

    @pl.when(ctx == 0)
    def _():
        def body(c, carry):
            anchor_copy(c).wait_send()
            return carry

        lax.fori_loop(1, n_ctx, body, 0)


def per_device(n_kv, n_ctx, hidden, w_query, w_key, w_value, keep_rows, keep_count):
    rows, depth = hidden.shape
    keep = keep_rows.shape[0]
    groups = w_query.shape[1] // HD
    nz = n_ctx // 4
    share = rows // n_ctx
    slots = keep + share
    freq = 500000.0 ** (-(np.arange(HD // 2, dtype=np.float64) * 2.0 / HD))
    freq = jnp.asarray(np.broadcast_to(np.concatenate([freq, freq]), (8, HD)), F32)
    any_spec = pl.BlockSpec(memory_space=pl.ANY)
    smem = pl.BlockSpec(memory_space=pltpu.SMEM)
    n_far = n_ctx * slots
    return pl.pallas_call(
        functools.partial(kernel, (rows, keep, share, groups, n_ctx, nz)),
        out_shape=jax.ShapeDtypeStruct((rows, groups * HD), BF),
        in_specs=[any_spec] * 4 + [smem, smem, any_spec],
        out_specs=any_spec,
        scratch_shapes=[
            pltpu.VMEM((n_kv, rows, depth), BF),
            pltpu.VMEM((n_kv, slots, depth), BF),
            pltpu.VMEM((n_kv * depth, (groups + 2) * HD), BF),
            pltpu.VMEM((2, nz, 2, slots, 2 * HD), BF),
            pltpu.VMEM((n_far, HD), BF),
            pltpu.VMEM((n_far, 2 * HD), BF),
            pltpu.VMEM((rows, HD), BF),
            pltpu.VMEM((rows, 2 * HD), BF),
            pltpu.VMEM((rows // 128, groups * 128, HD), BF),
            pltpu.VMEM((groups * 128, n_far + rows), F32),
            pltpu.VMEM((rows, HD), F32),
            pltpu.VMEM((rows, HD), F32),
            pltpu.VMEM((8, HD), F32),
            pltpu.VMEM((rows, groups * HD), BF),
            pltpu.SemaphoreType.DMA((96,)),
            pltpu.SemaphoreType.DMA((96,)),
            pltpu.SemaphoreType.DMA((n_ctx,)),
            pltpu.SemaphoreType.DMA,
            pltpu.SemaphoreType.DMA((16,)),
        ],
        compiler_params=pltpu.CompilerParams(
            collective_id=0, has_side_effects=True, vmem_limit_bytes=58 << 20
        ),
        name="prefill",
    )(hidden, w_query, w_key, w_value, keep_rows, keep_count, freq)


def solution(mesh):
    in_specs = (P("ctx", "kv"), P(None, "kv"), P(None, "kv"), P(None, "kv"), P("ctx"), P())
    out_specs = P("ctx", "kv")
    step = functools.partial(per_device, mesh.shape["kv"], mesh.shape["ctx"])
    return jax.shard_map(step, mesh=mesh, in_specs=in_specs, out_specs=out_specs, check_vma=False)
```

```python
import functools
import math

import jax
import jax.numpy as jnp
import numpy as np
from jax import lax
from jax.experimental import pallas as pl
from jax.experimental.pallas import tpu as pltpu
from jax.sharding import PartitionSpec as P

HD = 128
MESH = pl.DeviceIdType.MESH
BF = jnp.bfloat16
F32 = jnp.float32
SCALE = math.log2(math.e) / math.sqrt(HD)


def up16(n):
    return (n + 15) // 16 * 16


def send(part, dst, device, send_sem, recv_sem):
    copy = pltpu.make_async_remote_copy(
        src_ref=part, dst_ref=dst, send_sem=send_sem, recv_sem=recv_sem, device_id=device, device_id_type=MESH
    )
    copy.start()
    return copy


def take(like, sem):
    pltpu.make_async_copy(like, like, sem).wait()


class Gather:
    def __init__(self, sems, index, like, buf, base, rows, cut, kv_at, source):
        self.buf, self.base, self.rows, self.cut, self.at, self.source = buf, base, rows, cut, kv_at, source
        self.send_sem, self.recv = sems[0].at[index], [sems[1].at[index, i] for i in range(7)]
        self.like = like

    def part(self, dx, dy, lo, hi):
        return self.buf.at[self.at(dx, dy), pl.ds(self.base + lo, hi - lo)]

    def fwd(self, part, dx, dy, sem):
        return send(part, part, {"kv": self.at(dx, dy)}, self.send_sem, self.recv[sem])

    def own(self, ways=(0, 1, 2)):
        dst = self.part(0, 0, 0, self.rows)
        for i in ways:
            device = {"kv": self.at(*((1, 0), (3, 0), (0, 1))[i])}
            send(self.source, dst, device, self.send_sem, self.recv[i])

    def took(self, rows, sem):
        take(self.like.at[0, pl.ds(0, rows)], self.recv[sem])

    def second(self):
        n, cut, half = self.rows, self.cut, up16(self.rows // 2)
        self.took(n, 2)
        part = self.part(0, 1, cut, n)
        self.fwd(part, 1, 0, 3)
        self.fwd(part, 3, 0, 4)
        self.took(n, 0)
        self.fwd(self.part(3, 0, 0, half), 1, 0, 5)
        self.fwd(self.part(3, 0, 0, cut), 0, 1, 6)
        self.took(n, 1)
        self.fwd(self.part(1, 0, half, n), 3, 0, 5)
        self.fwd(self.part(1, 0, 0, cut), 0, 1, 6)

    def third(self):
        n, cut = self.rows, self.cut
        mid = cut + up16((n - cut) // 2)
        self.took(n - cut, 3)
        self.fwd(self.part(3, 1, cut, mid), 1, 0, 6)
        self.took(n - cut, 4)
        self.fwd(self.part(1, 1, mid, n), 3, 0, 6)
        self.took(n, 5)
        self.fwd(self.part(2, 0, 0, cut), 0, 1, 6)

    def finish(self):
        self.took(self.rows + 2 * self.cut, 6)

    def sent(self):
        take(self.like.at[0:7, pl.ds(0, self.rows)], self.send_sem)


def rope(field, cosine, sine):
    return field * cosine + pltpu.roll(field, HD // 2, 1) * sine


def tables(places, freq, sign):
    angles = places * freq
    return jnp.cos(angles), jnp.sin(angles) * sign


def lane_fold(op, s, total):
    for k in range(0, s.shape[1], HD):
        total = op(total, s[:, k : k + HD])
    return total


def kernel(
    sizes,
    hidden, w_query, w_key, w_value, keep_rows, keep_count, freq,
    out,
    H, RH, W, G, bias, KL, VL, Q, S, cos_t, sin_t, freq_v, out_v,
    k_send, k_recv, a_sem, c_send, c_recv, l_sem,
):
    rows, keep, share, groups, n_ctx, nz = sizes
    chunk = 128
    n_chunks = rows // chunk
    slots = keep + share
    depth = hidden.shape[1]
    n_src = H.shape[0]
    many = groups * chunk
    n_far = n_ctx * slots
    kv = lax.axis_index("kv")
    ctx = lax.axis_index("ctx")
    kx, ky = kv // 2, kv % 2
    yh, z, core = ctx // (2 * nz), (ctx // 2) % nz, ctx % 2

    def kv_at(dx, dy):
        return ((kx + dx) % 4) * 2 + (ky + dy) % 2

    def ctx_at(dy, dz, dc):
        return ((yh + dy) % 2) * (2 * nz) + ((z + dz) % nz) * 2 + (core + dc) % 2

    def fetch(src, dst, sem):
        copy = pltpu.make_async_copy(src, dst, l_sem.at[sem])
        copy.start()
        return copy

    barrier = pltpu.get_barrier_semaphore()
    kv_near = [(dx, dy) for dx in range(4) for dy in range(2) if dx or dy]
    ctx_near = ((1, 0, 0), (0, 1, 0), (0, nz - 1, 0), (0, 2, 0), (0, nz - 2, 0), (0, 0, 1))

    @pl.when(ctx != 0)
    def _():
        pl.semaphore_signal(barrier, inc=1, device_id={"ctx": 0}, device_id_type=MESH)

    for step in ctx_near:
        pl.semaphore_signal(barrier, inc=1, device_id={"ctx": ctx_at(*step)}, device_id_type=MESH)
    for step in kv_near:
        pl.semaphore_signal(barrier, inc=1, device_id={"kv": kv_at(*step)}, device_id_type=MESH)

    own_here = fetch(hidden, H.at[kv], 0)
    got_freq = fetch(freq, freq_v, 1)
    fetch(w_key, W.at[:, pl.ds(groups * HD, HD)], 2)
    fetch(w_value, W.at[:, pl.ds((groups + 1) * HD, HD)], 2)
    fetch(w_query, W.at[:, pl.ds(0, groups * HD)], 2)

    place_of = lax.broadcasted_iota(jnp.int32, (keep, HD), 0)
    picked = jnp.zeros((keep, HD), jnp.int32)
    for j in range(keep):
        picked = jnp.where(place_of == j, keep_rows[j], picked)
    lanes = lax.broadcasted_iota(jnp.int32, (keep, HD), 1)
    one_hot = jnp.concatenate(
        [(lanes + k * HD == picked).astype(F32).astype(BF) for k in range(rows // HD)], axis=1
    )
    own_here.wait()
    RH[kv, 0:keep] = jnp.dot(one_hot, H[kv], preferred_element_type=F32).astype(BF)

    near = len(kv_near) + len(ctx_near)
    pl.semaphore_wait(barrier, jnp.where(ctx == 0, near + n_ctx - 1, near))

    anchor_slot = RH.at[kv, pl.ds(keep, share)]

    def anchor_copy(c):
        return pltpu.make_async_remote_copy(
            src_ref=hidden.at[pl.ds(c * share, share)],
            dst_ref=anchor_slot,
            send_sem=a_sem.at[0],
            recv_sem=a_sem.at[1],
            device_id={"ctx": c},
            device_id_type=MESH,
        )

    @pl.when(ctx == 0)
    def _():
        def body(c, carry):
            anchor_copy(c).start()
            return carry

        lax.fori_loop(1, n_ctx, body, 0)
        mine = pltpu.make_async_copy(hidden.at[pl.ds(0, share)], anchor_slot, a_sem.at[1])
        mine.start()

    sems = (k_send, k_recv)
    extra = Gather(sems, n_chunks, H, RH, 0, keep, keep // 2, kv_at, RH.at[kv, pl.ds(0, keep)])
    parts = [
        Gather(sems, r, H, H, r * chunk, chunk, (48, 64)[r >= n_chunks // 2], kv_at, hidden.at[pl.ds(r * chunk, chunk)])
        for r in range(n_chunks)
    ]
    extra.own()

    KL[...] = jnp.zeros_like(KL)
    VL[...] = jnp.zeros_like(VL)
    row_of = lax.broadcasted_iota(jnp.int32, (slots, HD), 0)
    first_lane = lax.broadcasted_iota(jnp.int32, (slots, HD), 1) == 0

    def mark(i, carry):
        c = (i % 2) * (2 * nz) + ((i // 2) % nz) * 2 + i // (2 * nz)
        limit = jnp.where((c >= 1) & (c < ctx), keep_count[c], 0)
        anchors = jnp.where(ctx >= 1, slots, 0)
        live = row_of < jnp.where(row_of < keep, limit, anchors)
        at = pl.ds(pl.multiple_of(i * slots, 16), slots)
        bias[at, :] = jnp.where(first_lane & jnp.logical_not(live), -1e30, 0.0).astype(BF)
        return carry

    lax.fori_loop(0, n_ctx, mark, 0)

    extra.second()
    parts[0].own()

    got_freq.wait()
    freq_row = freq_v[0:1, :]
    lane = lax.broadcasted_iota(jnp.int32, (1, HD), 1)
    sign = jnp.where(lane < HD // 2, -1.0, 1.0)

    def table_of(i, carry):
        at = pl.ds(pl.multiple_of(i * 64, 64), 64)
        places = (ctx * rows + i * 64 + lax.broadcasted_iota(jnp.int32, (64, HD), 0)).astype(F32)
        cos_t[at, :], sin_t[at, :] = tables(places, freq_row, sign)
        return carry

    lax.fori_loop(0, rows // 64, table_of, 0)
    extra_places = jnp.concatenate(
        [
            (ctx * rows + picked).astype(F32),
            (ctx * share + lax.broadcasted_iota(jnp.int32, (share, HD), 0)).astype(F32),
        ],
        axis=0,
    )
    extra_cos, extra_sin = tables(extra_places, freq_row, sign)

    extra.third()
    anchor_copy(0).wait_recv()
    for step in kv_near:
        send(anchor_slot, anchor_slot, {"kv": kv_at(*step)}, a_sem.at[2], a_sem.at[3])
    parts[1].own((0, 1))
    parts[0].second()
    extra.finish()
    all_shares = H.at[0:7, pl.ds(0, share)]
    take(all_shares, a_sem.at[3])
    def block_at(at_z, at_y):
        return pl.ds(pl.multiple_of(((core * nz + at_z) * 2 + at_y) * slots, slots), slots)

    take(W, l_sem.at[2])
    kv_cols = slice(groups * HD, (groups + 2) * HD)
    raw = jnp.zeros((slots, 2 * HD), F32)
    for s in range(n_src):
        raw += jnp.dot(RH[s], W[s * depth : (s + 1) * depth, kv_cols], preferred_element_type=F32)
    own_block = block_at(z, yh)
    G[own_block, 0:HD] = rope(raw[:, :HD], extra_cos, extra_sin).astype(BF)
    G[own_block, HD:] = raw[:, HD:].astype(BF)

    def hop(part, step, send_sem, recv_sem):
        send(part, part, {"ctx": ctx_at(*step)}, c_send.at[send_sem], c_recv.at[recv_sem])

    def at_z(dz):
        return G.at[pl.ds(pl.multiple_of((core * nz + (z + dz) % nz) * 2 * slots, 2 * slots), 2 * slots)]

    def to_core(part):
        hop(part, (0, 0, 1), 2, 8)

    near_z = ((2, 1), (nz - 2, 2), (1, 3), (nz - 1, 4))
    block = G.at[own_block]
    hop(block, (1, 0, 0), 0, 0)
    for dz, sem in near_z:
        hop(block, (0, dz, 0), 1, sem)
    parts[1].own((2,))

    def project(r):
        part = pl.ds(pl.multiple_of(r * chunk, chunk), chunk)
        raw = jnp.zeros((chunk, (groups + 2) * HD), F32)
        for s in range(n_src):
            raw += jnp.dot(H[s, part], W[s * depth : (s + 1) * depth], preferred_element_type=F32)
        cosine, sine = cos_t[part, :], sin_t[part, :]
        for g in range(groups):
            at = pl.ds(pl.multiple_of(r * many + g * chunk, chunk), chunk)
            Q[at, :] = rope(raw[:, g * HD : (g + 1) * HD], cosine, sine).astype(BF)
        KL[part, :] = rope(raw[:, groups * HD : (groups + 1) * HD], cosine, sine).astype(BF)
        VL[part, :] = raw[:, (groups + 1) * HD :].astype(BF)

    take(block, c_recv.at[0])
    block = G.at[block_at(z, 1 - yh)]
    for dz, sem in near_z:
        hop(block, (0, dz, 0), 1, sem)
    to_core(at_z(0))
    parts[0].third()
    parts[2].own()
    parts[1].second()
    for i, (dz, sem) in enumerate(near_z):
        got = at_z(nz - dz)
        take(got, c_recv.at[sem])
        if i < 2:
            hop(got, (0, (1, nz - 1)[i], 0), 1, 5 + i)
            hop(G.at[block_at((z + nz - dz) % nz, i)], (0, dz, 0), 1, 7)
        to_core(got)
    parts[0].finish()
    project(0)
    parts[1].third()
    parts[3].own()
    for i, dz in enumerate((3, nz - 3)):
        got = at_z(nz - dz)
        take(got, c_recv.at[5 + i])
        to_core(got)
    got = at_z(nz // 2)
    take(got, c_recv.at[7])
    to_core(got)
    parts[2].second()
    parts[1].finish()
    project(1)
    half_far = n_far // 2
    take(G.at[0:half_far], c_recv.at[8])

    contract = (((1,), (1,)), ((), ()))
    in_chunk = lax.broadcasted_iota(jnp.int32, (many, rows), 0) % chunk
    key_place = lax.broadcasted_iota(jnp.int32, (many, rows), 1)
    adds_bias = (lax.broadcasted_iota(jnp.int32, (many, HD), 1) == 0).astype(F32).astype(BF)
    tile = 512
    tiles = range(0, n_far, tile)
    some = many // 2

    def attend(r):
        q = Q[pl.ds(pl.multiple_of(r * many, many), many), :]
        q_wide = jnp.concatenate([q, adds_bias], axis=1)
        s = lax.dot_general(q, KL[...], contract, preferred_element_type=F32)
        s = jnp.where(key_place <= in_chunk + r * chunk, s, -jnp.inf)
        S[:, n_far:] = s
        top = lane_fold(jnp.maximum, s[:, HD:], s[:, :HD])
        for at in tiles:
            keys = jnp.concatenate([G[at : at + tile, :HD], bias[at : at + tile]], axis=1)
            s = lax.dot_general(q_wide, keys, contract, preferred_element_type=F32)
            S[:, at : at + tile] = s
            top = lane_fold(jnp.maximum, s, top)
        top = jnp.max(top, axis=1, keepdims=True) * SCALE
        part = pl.ds(pl.multiple_of(r * chunk, chunk), chunk)
        for row in range(0, many, some):
            mine = slice(row, row + some)
            total = jnp.zeros((some, HD), F32)
            for at in range(0, n_far + rows, tile):
                e = jnp.exp2(S[mine, at : at + tile] * SCALE - top[mine])
                S[mine, at : at + tile] = e
                total = lane_fold(jnp.add, e, total)
            part_of = 1.0 / jnp.sum(total, axis=1, keepdims=True)
            result = jnp.zeros((some, HD), F32)
            for at in range(0, n_far + rows, tile):
                weights = (S[mine, at : at + tile] * part_of).astype(BF)
                values = G[at : at + tile, HD:] if at < n_far else VL[at - n_far : at - n_far + tile]
                result += jnp.dot(weights, values, preferred_element_type=F32)
            result = result.astype(BF)
            for g in range(some // chunk):
                head = row // chunk + g
                out_v[part, head * HD : (head + 1) * HD] = result[g * chunk : (g + 1) * chunk]
        fetch(out_v.at[part], out.at[part], 3)

    def step(r, carry):
        @pl.when(r == 1)
        def _():
            parts[2].third()
            parts[3].second()

        pl.when(r == 2)(parts[3].third)
        attend(r)

        @pl.when((r == 1) | (r == 2))
        def _():
            take(H.at[0, pl.ds(0, chunk + 2 * parts[3].cut)], k_recv.at[r + 1, 6])
            project(r + 1)

        return carry

    lax.fori_loop(0, n_chunks, step, 0)

    take(out_v, l_sem.at[3])
    for part in [extra, *parts]:
        part.sent()
    take(all_shares, a_sem.at[2])
    take(G.at[0:slots], c_send.at[0])
    take(G.at[0 : 14 * slots], c_send.at[1])
    take(G.at[0:half_far], c_send.at[2])

    @pl.when(ctx == 0)
    def _():
        take(H.at[0, pl.ds(0, (n_ctx - 1) * share)], a_sem.at[0])


def per_device(n_kv, n_ctx, hidden, w_query, w_key, w_value, keep_rows, keep_count):
    rows, depth = hidden.shape
    keep = keep_rows.shape[0]
    groups = w_query.shape[1] // HD
    nz = n_ctx // 4
    share = rows // n_ctx
    slots = keep + share
    freq = 500000.0 ** (-(np.arange(HD // 2, dtype=np.float64) * 2.0 / HD))
    freq = jnp.asarray(np.broadcast_to(np.concatenate([freq, freq]), (8, HD)), F32)
    any_spec = pl.BlockSpec(memory_space=pl.ANY)
    smem = pl.BlockSpec(memory_space=pltpu.SMEM)
    n_far = n_ctx * slots
    return pl.pallas_call(
        functools.partial(kernel, (rows, keep, share, groups, n_ctx, nz)),
        out_shape=jax.ShapeDtypeStruct((rows, groups * HD), BF),
        in_specs=[any_spec] * 4 + [smem, smem, any_spec],
        out_specs=any_spec,
        scratch_shapes=[
            pltpu.VMEM((n_kv, rows, depth), BF),
            pltpu.VMEM((n_kv, slots, depth), BF),
            pltpu.VMEM((n_kv * depth, (groups + 2) * HD), BF),
            pltpu.VMEM((n_far, 2 * HD), BF),
            pltpu.VMEM((n_far, HD), BF),
            pltpu.VMEM((rows, HD), BF),
            pltpu.VMEM((rows, HD), BF),
            pltpu.VMEM((rows * groups, HD), BF),
            pltpu.VMEM((groups * 128, n_far + rows), F32),
            pltpu.VMEM((rows, HD), F32),
            pltpu.VMEM((rows, HD), F32),
            pltpu.VMEM((8, HD), F32),
            pltpu.VMEM((rows, groups * HD), BF),
            pltpu.SemaphoreType.DMA((rows // 128 + 1,)),
            pltpu.SemaphoreType.DMA((rows // 128 + 1, 7)),
            pltpu.SemaphoreType.DMA((4,)),
            pltpu.SemaphoreType.DMA((3,)),
            pltpu.SemaphoreType.DMA((9,)),
            pltpu.SemaphoreType.DMA((4,)),
        ],
        compiler_params=pltpu.CompilerParams(
            collective_id=0, has_side_effects=True, vmem_limit_bytes=58 << 20
        ),
        name="prefill",
    )(hidden, w_query, w_key, w_value, keep_rows, keep_count, freq)


def solution(mesh):
    in_specs = (P("ctx", "kv"), P(None, "kv"), P(None, "kv"), P(None, "kv"), P("ctx"), P())
    out_specs = P("ctx", "kv")
    step = functools.partial(per_device, mesh.shape["kv"], mesh.shape["ctx"])
    return jax.shard_map(step, mesh=mesh, in_specs=in_specs, out_specs=out_specs, check_vma=False)
```

```python
import functools
import math

import jax
import jax.numpy as jnp
import numpy as np
from jax import lax
from jax.experimental import pallas as pl
from jax.experimental.pallas import tpu as pltpu
from jax.sharding import PartitionSpec as P

HD = 128
MESH = pl.DeviceIdType.MESH
BF = jnp.bfloat16
F32 = jnp.float32
SCALE = math.log2(math.e) / math.sqrt(HD)


def up16(n):
    return (n + 15) // 16 * 16


def send(part, dst, device, send_sem, recv_sem):
    copy = pltpu.make_async_remote_copy(
        src_ref=part, dst_ref=dst, send_sem=send_sem, recv_sem=recv_sem, device_id=device, device_id_type=MESH
    )
    copy.start()
    return copy


def take(like, sem):
    pltpu.make_async_copy(like, like, sem).wait()


class Gather:
    def __init__(self, sems, index, like, buf, base, rows, cut, kv_at, source):
        self.flip = index % 2
        self.buf, self.base, self.rows, self.cut, self.at, self.source = buf, base, rows, cut, kv_at, source
        self.send_sem, self.recv = sems[0].at[index], [sems[1].at[index, i] for i in range(7)]
        self.like = like

    def part(self, dx, dy, lo, hi):
        return self.buf.at[self.at(dx, dy), pl.ds(self.base + lo, hi - lo)]

    def fwd(self, part, dx, dy, sem):
        return send(part, part, {"kv": self.at(dx, dy)}, self.send_sem, self.recv[sem])

    def own(self, ways=(0, 1, 2)):
        dst = self.part(0, 0, 0, self.rows)
        for i in ways:
            device = {"kv": self.at(*((1, 0), (3, 0), (0, 1))[i])}
            send(self.source, dst, device, self.send_sem, self.recv[i])

    def took(self, rows, sem):
        take(self.like.at[0, pl.ds(0, rows)], self.recv[sem])

    def second(self):
        n, cut, half = self.rows, self.cut, up16(self.rows // 2)
        self.took(n, 2)
        part = self.part(0, 1, cut, n)
        self.fwd(part, 1, 0, 3)
        self.fwd(part, 3, 0, 4)
        self.took(n, 0)
        self.fwd(self.part(3, 0, 0, half), 1, 0, 5)
        self.fwd(self.part(3, 0, 0, cut), 0, 1, 6)
        self.took(n, 1)
        self.fwd(self.part(1, 0, half, n), 3, 0, 5)
        self.fwd(self.part(1, 0, 0, cut), 0, 1, 6)

    def third(self):
        n, cut = self.rows, self.cut
        mid = cut + up16((n - cut) // 2)
        if self.flip:
            mid = n + cut - mid
        self.took(n - cut, 3)
        self.fwd(self.part(3, 1, cut, mid), 1, 0, 6)
        self.took(n - cut, 4)
        self.fwd(self.part(1, 1, mid, n), 3, 0, 6)
        self.took(n, 5)
        self.fwd(self.part(2, 0, 0, cut), 0, 1, 6)

    def finish(self):
        self.took(self.rows + 2 * self.cut, 6)

    def sent(self):
        take(self.like.at[0:7, pl.ds(0, self.rows)], self.send_sem)


def rope(field, cosine, sine):
    return field * cosine + pltpu.roll(field, HD // 2, 1) * sine


def tables(places, freq, sign):
    angles = places * freq
    return jnp.cos(angles), jnp.sin(angles) * sign


def lane_fold(op, s, total):
    for k in range(0, s.shape[1], HD):
        total = op(total, s[:, k : k + HD])
    return total


def kernel(
    sizes,
    hidden, w_query, w_key, w_value, keep_rows, keep_count, freq,
    out,
    H, RH, W, G, bias, KL, VL, Q, S, cos_t, sin_t, freq_v, out_v,
    k_send, k_recv, a_sem, c_send, c_recv, l_sem,
):
    rows, keep, share, groups, n_ctx, nz = sizes
    chunk = 128
    n_chunks = rows // chunk
    slots = keep + share
    depth = hidden.shape[1]
    n_src = H.shape[0]
    many = groups * chunk
    n_far = n_ctx * slots
    kv = lax.axis_index("kv")
    ctx = lax.axis_index("ctx")
    kx, ky = kv // 2, kv % 2
    yh, z, core = ctx // (2 * nz), (ctx // 2) % nz, ctx % 2

    def kv_at(dx, dy):
        return ((kx + dx) % 4) * 2 + (ky + dy) % 2

    def ctx_at(dy, dz, dc):
        return ((yh + dy) % 2) * (2 * nz) + ((z + dz) % nz) * 2 + (core + dc) % 2

    def fetch(src, dst, sem):
        copy = pltpu.make_async_copy(src, dst, l_sem.at[sem])
        copy.start()
        return copy

    barrier = pltpu.get_barrier_semaphore()
    kv_near = [(dx, dy) for dx in range(4) for dy in range(2) if dx or dy]
    ctx_near = ((1, 0, 0), (0, 1, 0), (0, nz - 1, 0), (0, 2, 0), (0, nz - 2, 0), (0, 0, 1))

    @pl.when(ctx != 0)
    def _():
        pl.semaphore_signal(barrier, inc=1, device_id={"ctx": 0}, device_id_type=MESH)

    for step in ctx_near:
        pl.semaphore_signal(barrier, inc=1, device_id={"ctx": ctx_at(*step)}, device_id_type=MESH)
    for step in kv_near:
        pl.semaphore_signal(barrier, inc=1, device_id={"kv": kv_at(*step)}, device_id_type=MESH)

    own_here = fetch(hidden, H.at[kv], 0)
    got_freq = fetch(freq, freq_v, 1)
    fetch(w_key, W.at[:, pl.ds(groups * HD, HD)], 2)
    fetch(w_value, W.at[:, pl.ds((groups + 1) * HD, HD)], 2)
    fetch(w_query, W.at[:, pl.ds(0, groups * HD)], 2)

    place_of = lax.broadcasted_iota(jnp.int32, (keep, HD), 0)
    picked = jnp.zeros((keep, HD), jnp.int32)
    for j in range(keep):
        picked = jnp.where(place_of == j, keep_rows[j], picked)
    lanes = lax.broadcasted_iota(jnp.int32, (keep, HD), 1)
    one_hot = jnp.concatenate(
        [(lanes + k * HD == picked).astype(F32).astype(BF) for k in range(rows // HD)], axis=1
    )
    own_here.wait()

    has_extra = ctx != 0

    @pl.when(has_extra)
    def _():
        RH[kv, 0:keep] = jnp.dot(one_hot, H[kv], preferred_element_type=F32).astype(BF)

    @pl.when(ctx == 0)
    def _():
        RH[:, 0:keep] = jnp.zeros((n_src, keep, depth), BF)


    near = len(kv_near) + len(ctx_near)
    pl.semaphore_wait(barrier, jnp.where(ctx == 0, near + n_ctx - 1, near))

    anchor_slot = RH.at[kv, pl.ds(keep, share)]

    def anchor_copy(c):
        return pltpu.make_async_remote_copy(
            src_ref=hidden.at[pl.ds(c * share, share)],
            dst_ref=anchor_slot,
            send_sem=a_sem.at[0],
            recv_sem=a_sem.at[1],
            device_id={"ctx": c},
            device_id_type=MESH,
        )

    @pl.when(ctx == 0)
    def _():
        def body(c, carry):
            anchor_copy(c).start()
            return carry

        lax.fori_loop(1, n_ctx, body, 0)
        mine = pltpu.make_async_copy(hidden.at[pl.ds(0, share)], anchor_slot, a_sem.at[1])
        mine.start()

    sems = (k_send, k_recv)
    extra = Gather(sems, n_chunks, H, RH, 0, keep, keep // 2, kv_at, RH.at[kv, pl.ds(0, keep)])
    parts = [
        Gather(sems, r, H, H, r * chunk, chunk, (48 if r else 64), kv_at, hidden.at[pl.ds(r * chunk, chunk)])
        for r in range(n_chunks)
    ]
    pl.when(has_extra)(extra.own)

    KL[...] = jnp.zeros_like(KL)
    VL[...] = jnp.zeros_like(VL)
    row_of = lax.broadcasted_iota(jnp.int32, (slots, HD), 0)
    first_lane = lax.broadcasted_iota(jnp.int32, (slots, HD), 1) == 0

    def mark(i, carry):
        c = (i % 2) * (2 * nz) + ((i // 2) % nz) * 2 + i // (2 * nz)
        limit = jnp.where((c >= 1) & (c < ctx), keep_count[c], 0)
        anchors = jnp.where(ctx >= 1, slots, 0)
        live = row_of < jnp.where(row_of < keep, limit, anchors)
        at = pl.ds(pl.multiple_of(i * slots, 16), slots)
        bias[at, :] = jnp.where(first_lane & jnp.logical_not(live), -1e30, 0.0).astype(BF)
        return carry

    lax.fori_loop(0, n_ctx, mark, 0)

    pl.when(has_extra)(extra.second)
    parts[0].own()

    got_freq.wait()
    freq_row = freq_v[0:1, :]
    lane = lax.broadcasted_iota(jnp.int32, (1, HD), 1)
    sign = jnp.where(lane < HD // 2, -1.0, 1.0)

    def table_of(i, carry):
        at = pl.ds(pl.multiple_of(i * 64, 64), 64)
        places = (ctx * rows + i * 64 + lax.broadcasted_iota(jnp.int32, (64, HD), 0)).astype(F32)
        cos_t[at, :], sin_t[at, :] = tables(places, freq_row, sign)
        return carry

    lax.fori_loop(0, rows // 64, table_of, 0)
    extra_places = jnp.concatenate(
        [
            (ctx * rows + picked).astype(F32),
            (ctx * share + lax.broadcasted_iota(jnp.int32, (share, HD), 0)).astype(F32),
        ],
        axis=0,
    )
    extra_cos, extra_sin = tables(extra_places, freq_row, sign)

    pl.when(has_extra)(extra.third)
    anchor_copy(0).wait_recv()
    for step in kv_near:
        send(anchor_slot, anchor_slot, {"kv": kv_at(*step)}, a_sem.at[2], a_sem.at[3])
    parts[1].own((0, 1))
    parts[0].second()
    pl.when(has_extra)(extra.finish)
    all_shares = H.at[0:7, pl.ds(0, share)]
    take(all_shares, a_sem.at[3])
    def block_at(at_z, at_y):
        return pl.ds(pl.multiple_of(((core * nz + at_z) * 2 + at_y) * slots, slots), slots)

    take(W, l_sem.at[2])
    kv_cols = slice(groups * HD, (groups + 2) * HD)
    raw = jnp.zeros((slots, 2 * HD), F32)
    for s in range(n_src):
        raw += jnp.dot(RH[s], W[s * depth : (s + 1) * depth, kv_cols], preferred_element_type=F32)
    own_block = block_at(z, yh)
    G[own_block, 0:HD] = rope(raw[:, :HD], extra_cos, extra_sin).astype(BF)
    G[own_block, HD:] = raw[:, HD:].astype(BF)

    def hop(part, step, send_sem, recv_sem):
        send(part, part, {"ctx": ctx_at(*step)}, c_send.at[send_sem], c_recv.at[recv_sem])

    def at_z(dz):
        return G.at[pl.ds(pl.multiple_of((core * nz + (z + dz) % nz) * 2 * slots, 2 * slots), 2 * slots)]

    def to_core(part):
        hop(part, (0, 0, 1), 2, 8)

    near_z = ((2, 1, 9), (nz - 2, 2, 10), (1, 3, 3), (nz - 1, 4, 4))
    block = G.at[own_block]
    hop(block, (1, 0, 0), 0, 0)
    for dz, sem, _ in near_z:
        hop(block, (0, dz, 0), 1, sem)
    parts[1].own((2,))

    def project(r):
        part = pl.ds(pl.multiple_of(r * chunk, chunk), chunk)
        raw = jnp.zeros((chunk, (groups + 2) * HD), F32)
        for s in range(n_src):
            raw += jnp.dot(H[s, part], W[s * depth : (s + 1) * depth], preferred_element_type=F32)
        cosine, sine = cos_t[part, :], sin_t[part, :]
        for g in range(groups):
            at = pl.ds(pl.multiple_of(r * many + g * chunk, chunk), chunk)
            Q[at, :] = rope(raw[:, g * HD : (g + 1) * HD], cosine, sine).astype(BF)
        KL[part, :] = rope(raw[:, groups * HD : (groups + 1) * HD], cosine, sine).astype(BF)
        VL[part, :] = raw[:, (groups + 1) * HD :].astype(BF)

    take(block, c_recv.at[0])
    block = G.at[block_at(z, 1 - yh)]
    for dz, _, sem in near_z:
        hop(block, (0, dz, 0), 1, sem)
    to_core(at_z(0))

    def onward(which):
        at_y = (yh, 1 - yh)[which]
        for i, (dz, *sems_z) in enumerate(near_z[:2]):
            got = G.at[block_at((z + nz - dz) % nz, at_y)]
            take(got, c_recv.at[sems_z[which]])
            hop(got, (0, (1, nz - 1)[i], 0), 1, 5 + i)
            if i == which:
                hop(got, (0, dz, 0), 1, 7)

    onward(0)
    parts[0].third()
    parts[2].own()
    parts[1].second()
    onward(1)
    for dz, _, sem in near_z:
        got = at_z(nz - dz)
        if dz in (1, nz - 1):
            take(got, c_recv.at[sem])
        to_core(got)
    parts[3].own()
    for i, dz in enumerate((3, nz - 3)):
        got = at_z(nz - dz)
        take(got, c_recv.at[5 + i])
        to_core(got)
    got = at_z(nz // 2)
    take(got, c_recv.at[7])
    to_core(got)
    parts[1].third()
    parts[0].finish()
    project(0)
    parts[2].second()
    half_far = n_far // 2
    take(G.at[0:half_far], c_recv.at[8])

    contract = (((1,), (1,)), ((), ()))
    in_chunk = lax.broadcasted_iota(jnp.int32, (many, rows), 0) % chunk
    key_place = lax.broadcasted_iota(jnp.int32, (many, rows), 1)
    adds_bias = (lax.broadcasted_iota(jnp.int32, (many, HD), 1) == 0).astype(F32).astype(BF)
    tile = 512
    tiles = range(0, n_far, tile)
    some = many // 2

    def attend(r):
        q = Q[pl.ds(pl.multiple_of(r * many, many), many), :]
        q_wide = jnp.concatenate([q, adds_bias], axis=1)
        s = lax.dot_general(q, KL[...], contract, preferred_element_type=F32)
        s = jnp.where(key_place <= in_chunk + r * chunk, s, -jnp.inf)
        S[:, n_far:] = s
        top = lane_fold(jnp.maximum, s[:, HD:], s[:, :HD])
        for at in tiles:
            keys = jnp.concatenate([G[at : at + tile, :HD], bias[at : at + tile]], axis=1)
            s = lax.dot_general(q_wide, keys, contract, preferred_element_type=F32)
            S[:, at : at + tile] = s
            top = lane_fold(jnp.maximum, s, top)
        top = jnp.max(top, axis=1, keepdims=True) * SCALE
        part = pl.ds(pl.multiple_of(r * chunk, chunk), chunk)
        for row in range(0, many, some):
            mine = slice(row, row + some)
            total = jnp.zeros((some, HD), F32)
            for at in range(0, n_far + rows, tile):
                e = jnp.exp2(S[mine, at : at + tile] * SCALE - top[mine])
                S[mine, at : at + tile] = e
                total = lane_fold(jnp.add, e, total)
            part_of = 1.0 / jnp.sum(total, axis=1, keepdims=True)
            result = jnp.zeros((some, HD), F32)
            for at in range(0, n_far + rows, tile):
                weights = (S[mine, at : at + tile] * part_of).astype(BF)
                values = G[at : at + tile, HD:] if at < n_far else VL[at - n_far : at - n_far + tile]
                result += jnp.dot(weights, values, preferred_element_type=F32)
            result = result.astype(BF)
            for g in range(some // chunk):
                head = row // chunk + g
                out_v[part, head * HD : (head + 1) * HD] = result[g * chunk : (g + 1) * chunk]
        fetch(out_v.at[part], out.at[part], 3)

    def step(r, carry):
        attend(r)

        @pl.when(r == 0)
        def _():
            parts[2].third()
            parts[3].second()

        pl.when(r == 1)(parts[3].third)

        @pl.when(r < n_chunks - 1)
        def _():
            take(H.at[0, pl.ds(0, chunk + 2 * parts[3].cut)], k_recv.at[r + 1, 6])
            project(r + 1)

        return carry

    lax.fori_loop(0, n_chunks, step, 0)

    take(out_v, l_sem.at[3])
    pl.when(has_extra)(extra.sent)
    for part in parts:
        part.sent()
    take(all_shares, a_sem.at[2])
    take(G.at[0:slots], c_send.at[0])
    take(G.at[0 : 14 * slots], c_send.at[1])
    take(G.at[0:half_far], c_send.at[2])

    @pl.when(ctx == 0)
    def _():
        take(H.at[0, pl.ds(0, (n_ctx - 1) * share)], a_sem.at[0])


def per_device(n_kv, n_ctx, hidden, w_query, w_key, w_value, keep_rows, keep_count):
    rows, depth = hidden.shape
    keep = keep_rows.shape[0]
    groups = w_query.shape[1] // HD
    nz = n_ctx // 4
    share = rows // n_ctx
    slots = keep + share
    freq = 500000.0 ** (-(np.arange(HD // 2, dtype=np.float64) * 2.0 / HD))
    freq = jnp.asarray(np.broadcast_to(np.concatenate([freq, freq]), (8, HD)), F32)
    any_spec = pl.BlockSpec(memory_space=pl.ANY)
    smem = pl.BlockSpec(memory_space=pltpu.SMEM)
    n_far = n_ctx * slots
    return pl.pallas_call(
        functools.partial(kernel, (rows, keep, share, groups, n_ctx, nz)),
        out_shape=jax.ShapeDtypeStruct((rows, groups * HD), BF),
        in_specs=[any_spec] * 4 + [smem, smem, any_spec],
        out_specs=any_spec,
        scratch_shapes=[
            pltpu.VMEM((n_kv, rows, depth), BF),
            pltpu.VMEM((n_kv, slots, depth), BF),
            pltpu.VMEM((n_kv * depth, (groups + 2) * HD), BF),
            pltpu.VMEM((n_far, 2 * HD), BF),
            pltpu.VMEM((n_far, HD), BF),
            pltpu.VMEM((rows, HD), BF),
            pltpu.VMEM((rows, HD), BF),
            pltpu.VMEM((rows * groups, HD), BF),
            pltpu.VMEM((groups * 128, n_far + rows), F32),
            pltpu.VMEM((rows, HD), F32),
            pltpu.VMEM((rows, HD), F32),
            pltpu.VMEM((8, HD), F32),
            pltpu.VMEM((rows, groups * HD), BF),
            pltpu.SemaphoreType.DMA((rows // 128 + 1,)),
            pltpu.SemaphoreType.DMA((rows // 128 + 1, 7)),
            pltpu.SemaphoreType.DMA((4,)),
            pltpu.SemaphoreType.DMA((3,)),
            pltpu.SemaphoreType.DMA((11,)),
            pltpu.SemaphoreType.DMA((4,)),
        ],
        compiler_params=pltpu.CompilerParams(
            collective_id=0, has_side_effects=True, vmem_limit_bytes=58 << 20
        ),
        name="prefill",
    )(hidden, w_query, w_key, w_value, keep_rows, keep_count, freq)


def solution(mesh):
    in_specs = (P("ctx", "kv"), P(None, "kv"), P(None, "kv"), P(None, "kv"), P("ctx"), P())
    out_specs = P("ctx", "kv")
    step = functools.partial(per_device, mesh.shape["kv"], mesh.shape["ctx"])
    return jax.shard_map(step, mesh=mesh, in_specs=in_specs, out_specs=out_specs, check_vma=False)
```

```python
import functools
import math

import jax
import jax.numpy as jnp
import numpy as np
from jax import lax
from jax.experimental import pallas as pl
from jax.experimental.pallas import tpu as pltpu
from jax.sharding import PartitionSpec as P

HD = 128
MESH = pl.DeviceIdType.MESH
BF = jnp.bfloat16
F32 = jnp.float32
SCALE = math.log2(math.e) / math.sqrt(HD)


def up16(n):
    return (n + 15) // 16 * 16


def send(part, dst, device, send_sem, recv_sem):
    copy = pltpu.make_async_remote_copy(
        src_ref=part, dst_ref=dst, send_sem=send_sem, recv_sem=recv_sem, device_id=device, device_id_type=MESH
    )
    copy.start()
    return copy


def take(like, sem):
    pltpu.make_async_copy(like, like, sem).wait()


class Gather:
    def __init__(self, sems, index, like, buf, base, rows, cut, kv_at, source):
        self.flip = index % 2
        self.buf, self.base, self.rows, self.cut, self.at, self.source = buf, base, rows, cut, kv_at, source
        self.send_sem, self.recv = sems[0].at[index], [sems[1].at[index, i] for i in range(7)]
        self.like = like

    def part(self, dx, dy, lo, hi):
        return self.buf.at[self.at(dx, dy), pl.ds(self.base + lo, hi - lo)]

    def fwd(self, part, dx, dy, sem):
        return send(part, part, {"kv": self.at(dx, dy)}, self.send_sem, self.recv[sem])

    def own(self, ways=(0, 1, 2)):
        dst = self.part(0, 0, 0, self.rows)
        for i in ways:
            device = {"kv": self.at(*((1, 0), (3, 0), (0, 1))[i])}
            send(self.source, dst, device, self.send_sem, self.recv[i])

    def took(self, rows, sem):
        take(self.like.at[0, pl.ds(0, rows)], self.recv[sem])

    def second(self):
        n, cut, half = self.rows, self.cut, up16(self.rows // 2)
        self.took(n, 2)
        part = self.part(0, 1, cut, n)
        self.fwd(part, 1, 0, 3)
        self.fwd(part, 3, 0, 4)
        self.took(n, 0)
        self.fwd(self.part(3, 0, 0, half), 1, 0, 5)
        self.fwd(self.part(3, 0, 0, cut), 0, 1, 6)
        self.took(n, 1)
        self.fwd(self.part(1, 0, half, n), 3, 0, 5)
        self.fwd(self.part(1, 0, 0, cut), 0, 1, 6)

    def third(self):
        n, cut = self.rows, self.cut
        mid = cut + up16((n - cut) // 2)
        if self.flip:
            mid = n + cut - mid
        self.took(n - cut, 3)
        self.fwd(self.part(3, 1, cut, mid), 1, 0, 6)
        self.took(n - cut, 4)
        self.fwd(self.part(1, 1, mid, n), 3, 0, 6)
        self.took(n, 5)
        self.fwd(self.part(2, 0, 0, cut), 0, 1, 6)

    def finish(self):
        self.took(self.rows + 2 * self.cut, 6)

    def sent(self):
        take(self.like.at[0:7, pl.ds(0, self.rows)], self.send_sem)


def rope(field, cosine, sine):
    return field * cosine + pltpu.roll(field, HD // 2, 1) * sine


def tables(places, freq, sign):
    angles = places * freq
    return jnp.cos(angles), jnp.sin(angles) * sign


def lane_fold(op, s, total):
    for k in range(0, s.shape[1], HD):
        total = op(total, s[:, k : k + HD])
    return total


def kernel(
    sizes,
    hidden, w_query, w_key, w_value, keep_rows, keep_count, freq,
    out,
    H, RH, W, G, bias, KL, VL, Q, S, cos_t, sin_t, freq_v, out_v,
    k_send, k_recv, a_sem, c_send, c_recv, l_sem,
):
    rows, keep, share, groups, n_ctx, nz = sizes
    chunk = 128
    n_chunks = rows // chunk
    slots = keep + share
    depth = hidden.shape[1]
    n_src = H.shape[0]
    many = groups * chunk
    n_far = n_ctx * slots
    kv = lax.axis_index("kv")
    ctx = lax.axis_index("ctx")
    kx, ky = kv // 2, kv % 2
    yh, z, core = ctx // (2 * nz), (ctx // 2) % nz, ctx % 2

    def kv_at(dx, dy):
        return ((kx + dx) % 4) * 2 + (ky + dy) % 2

    def ctx_at(dy, dz, dc):
        return ((yh + dy) % 2) * (2 * nz) + ((z + dz) % nz) * 2 + (core + dc) % 2

    def fetch(src, dst, sem):
        copy = pltpu.make_async_copy(src, dst, l_sem.at[sem])
        copy.start()
        return copy

    barrier = pltpu.get_barrier_semaphore()
    kv_near = [(dx, dy) for dx in range(4) for dy in range(2) if dx or dy]
    ctx_near = ((1, 0, 0), (0, 1, 0), (0, nz - 1, 0), (0, 2, 0), (0, nz - 2, 0), (0, 0, 1))

    @pl.when(ctx != 0)
    def _():
        pl.semaphore_signal(barrier, inc=1, device_id={"ctx": 0}, device_id_type=MESH)

    for step in ctx_near:
        pl.semaphore_signal(barrier, inc=1, device_id={"ctx": ctx_at(*step)}, device_id_type=MESH)
    for step in kv_near:
        pl.semaphore_signal(barrier, inc=1, device_id={"kv": kv_at(*step)}, device_id_type=MESH)

    own_here = fetch(hidden, H.at[kv], 0)
    got_freq = fetch(freq, freq_v, 1)
    fetch(w_key, W.at[:, pl.ds(groups * HD, HD)], 2)
    fetch(w_value, W.at[:, pl.ds((groups + 1) * HD, HD)], 2)
    fetch(w_query, W.at[:, pl.ds(0, groups * HD)], 2)

    place_of = lax.broadcasted_iota(jnp.int32, (keep, HD), 0)
    picked = jnp.zeros((keep, HD), jnp.int32)
    for j in range(keep):
        picked = jnp.where(place_of == j, keep_rows[j], picked)
    lanes = lax.broadcasted_iota(jnp.int32, (keep, HD), 1)
    one_hot = jnp.concatenate(
        [(lanes + k * HD == picked).astype(F32).astype(BF) for k in range(rows // HD)], axis=1
    )
    own_here.wait()

    has_extra = ctx != 0

    @pl.when(has_extra)
    def _():
        RH[kv, 0:keep] = jnp.dot(one_hot, H[kv], preferred_element_type=F32).astype(BF)

    @pl.when(ctx == 0)
    def _():
        RH[:, 0:keep] = jnp.zeros((n_src, keep, depth), BF)


    near = len(kv_near) + len(ctx_near)
    pl.semaphore_wait(barrier, jnp.where(ctx == 0, near + n_ctx - 1, near))

    anchor_slot = RH.at[kv, pl.ds(keep, share)]

    def anchor_copy(c):
        return pltpu.make_async_remote_copy(
            src_ref=hidden.at[pl.ds(c * share, share)],
            dst_ref=anchor_slot,
            send_sem=a_sem.at[0],
            recv_sem=a_sem.at[1],
            device_id={"ctx": c},
            device_id_type=MESH,
        )

    @pl.when(ctx == 0)
    def _():
        def body(c, carry):
            anchor_copy(c).start()
            return carry

        lax.fori_loop(1, n_ctx, body, 0)
        mine = pltpu.make_async_copy(hidden.at[pl.ds(0, share)], anchor_slot, a_sem.at[1])
        mine.start()

    sems = (k_send, k_recv)
    extra = Gather(sems, n_chunks, H, RH, 0, keep, keep // 2, kv_at, RH.at[kv, pl.ds(0, keep)])
    parts = [
        Gather(sems, r, H, H, r * chunk, chunk, (48 if r else 64), kv_at, hidden.at[pl.ds(r * chunk, chunk)])
        for r in range(n_chunks)
    ]
    pl.when(has_extra)(extra.own)

    KL[...] = jnp.zeros_like(KL)
    VL[...] = jnp.zeros_like(VL)
    row_of = lax.broadcasted_iota(jnp.int32, (slots, HD), 0)
    first_lane = lax.broadcasted_iota(jnp.int32, (slots, HD), 1) == 0

    def mark(i, carry):
        c = (i % 2) * (2 * nz) + ((i // 2) % nz) * 2 + i // (2 * nz)
        limit = jnp.where((c >= 1) & (c < ctx), keep_count[c], 0)
        anchors = jnp.where(ctx >= 1, slots, 0)
        live = row_of < jnp.where(row_of < keep, limit, anchors)
        at = pl.ds(pl.multiple_of(i * slots, 16), slots)
        bias[at, :] = jnp.where(first_lane & jnp.logical_not(live), -1e30, 0.0).astype(BF)
        return carry

    lax.fori_loop(0, n_ctx, mark, 0)

    pl.when(has_extra)(extra.second)
    parts[0].own()

    got_freq.wait()
    freq_row = freq_v[0:1, :]
    lane = lax.broadcasted_iota(jnp.int32, (1, HD), 1)
    sign = jnp.where(lane < HD // 2, -1.0, 1.0)

    def table_of(i, carry):
        at = pl.ds(pl.multiple_of(i * 64, 64), 64)
        places = (ctx * rows + i * 64 + lax.broadcasted_iota(jnp.int32, (64, HD), 0)).astype(F32)
        cos_t[at, :], sin_t[at, :] = tables(places, freq_row, sign)
        return carry

    lax.fori_loop(0, rows // 64, table_of, 0)
    extra_places = jnp.concatenate(
        [
            (ctx * rows + picked).astype(F32),
            (ctx * share + lax.broadcasted_iota(jnp.int32, (share, HD), 0)).astype(F32),
        ],
        axis=0,
    )
    extra_cos, extra_sin = tables(extra_places, freq_row, sign)

    pl.when(has_extra)(extra.third)
    anchor_copy(0).wait_recv()
    for step in kv_near:
        send(anchor_slot, anchor_slot, {"kv": kv_at(*step)}, a_sem.at[2], a_sem.at[3])
    parts[1].own((0, 1))
    parts[0].second()
    pl.when(has_extra)(extra.finish)
    all_shares = H.at[0:7, pl.ds(0, share)]
    take(all_shares, a_sem.at[3])
    def block_at(at_z, at_y):
        return pl.ds(pl.multiple_of(((core * nz + at_z) * 2 + at_y) * slots, slots), slots)

    take(W, l_sem.at[2])
    kv_cols = slice(groups * HD, (groups + 2) * HD)
    raw = jnp.zeros((slots, 2 * HD), F32)
    for s in range(n_src):
        raw += jnp.dot(RH[s], W[s * depth : (s + 1) * depth, kv_cols], preferred_element_type=F32)
    own_block = block_at(z, yh)
    G[own_block, 0:HD] = rope(raw[:, :HD], extra_cos, extra_sin).astype(BF)
    G[own_block, HD:] = raw[:, HD:].astype(BF)

    def hop(part, step, send_sem, recv_sem):
        send(part, part, {"ctx": ctx_at(*step)}, c_send.at[send_sem], c_recv.at[recv_sem])

    def at_z(dz):
        return G.at[pl.ds(pl.multiple_of((core * nz + (z + dz) % nz) * 2 * slots, 2 * slots), 2 * slots)]

    def to_core(part):
        hop(part, (0, 0, 1), 2, 8)

    near_z = ((2, 1, 9), (nz - 2, 2, 10), (1, 3, 3), (nz - 1, 4, 4))
    block = G.at[own_block]
    hop(block, (1, 0, 0), 0, 0)
    for dz, sem, _ in near_z:
        hop(block, (0, dz, 0), 1, sem)
    parts[1].own((2,))

    def project(r):
        part = pl.ds(pl.multiple_of(r * chunk, chunk), chunk)
        raw = jnp.zeros((chunk, (groups + 2) * HD), F32)
        for s in range(n_src):
            raw += jnp.dot(H[s, part], W[s * depth : (s + 1) * depth], preferred_element_type=F32)
        cosine, sine = cos_t[part, :], sin_t[part, :]
        for g in range(groups):
            at = pl.ds(pl.multiple_of(r * many + g * chunk, chunk), chunk)
            Q[at, :] = rope(raw[:, g * HD : (g + 1) * HD], cosine, sine).astype(BF)
        KL[part, :] = rope(raw[:, groups * HD : (groups + 1) * HD], cosine, sine).astype(BF)
        VL[part, :] = raw[:, (groups + 1) * HD :].astype(BF)

    take(block, c_recv.at[0])
    block = G.at[block_at(z, 1 - yh)]
    for dz, _, sem in near_z:
        hop(block, (0, dz, 0), 1, sem)
    to_core(at_z(0))

    def onward(which):
        at_y = (yh, 1 - yh)[which]
        for i, (dz, *sems_z) in enumerate(near_z[:2]):
            got = G.at[block_at((z + nz - dz) % nz, at_y)]
            take(got, c_recv.at[sems_z[which]])
            hop(got, (0, (1, nz - 1)[i], 0), 1, 5 + i)
            if i == which:
                hop(got, (0, dz, 0), 1, 7)

    onward(0)
    parts[0].third()
    parts[2].own()
    parts[1].second()
    parts[3].own()
    onward(1)
    for dz, _, sem in near_z:
        got = at_z(nz - dz)
        if dz in (1, nz - 1):
            take(got, c_recv.at[sem])
        to_core(got)
    parts[0].finish()
    project(0)
    for i, dz in enumerate((3, nz - 3)):
        got = at_z(nz - dz)
        take(got, c_recv.at[5 + i])
        to_core(got)
    got = at_z(nz // 2)
    take(got, c_recv.at[7])
    to_core(got)
    parts[1].third()
    parts[2].second()
    parts[3].second()
    half_far = n_far // 2
    take(G.at[0:half_far], c_recv.at[8])

    contract = (((1,), (1,)), ((), ()))
    in_chunk = lax.broadcasted_iota(jnp.int32, (many, rows), 0) % chunk
    key_place = lax.broadcasted_iota(jnp.int32, (many, rows), 1)
    adds_bias = (lax.broadcasted_iota(jnp.int32, (many, HD), 1) == 0).astype(F32).astype(BF)
    tile = 512
    tiles = range(0, n_far, tile)
    some = many // 2

    def attend(r):
        q = Q[pl.ds(pl.multiple_of(r * many, many), many), :]
        q_wide = jnp.concatenate([q, adds_bias], axis=1)
        s = lax.dot_general(q, KL[...], contract, preferred_element_type=F32)
        s = jnp.where(key_place <= in_chunk + r * chunk, s, -jnp.inf)
        S[:, n_far:] = s
        top = lane_fold(jnp.maximum, s[:, HD:], s[:, :HD])
        for at in tiles:
            keys = jnp.concatenate([G[at : at + tile, :HD], bias[at : at + tile]], axis=1)
            s = lax.dot_general(q_wide, keys, contract, preferred_element_type=F32)
            S[:, at : at + tile] = s
            top = lane_fold(jnp.maximum, s, top)
        top = jnp.max(top, axis=1, keepdims=True) * SCALE
        part = pl.ds(pl.multiple_of(r * chunk, chunk), chunk)
        for row in range(0, many, some):
            mine = slice(row, row + some)
            total = jnp.zeros((some, HD), F32)
            for at in range(0, n_far + rows, tile):
                e = jnp.exp2(S[mine, at : at + tile] * SCALE - top[mine])
                S[mine, at : at + tile] = e
                total = lane_fold(jnp.add, e, total)
            part_of = 1.0 / jnp.sum(total, axis=1, keepdims=True)
            result = jnp.zeros((some, HD), F32)
            for at in range(0, n_far + rows, tile):
                weights = (S[mine, at : at + tile] * part_of).astype(BF)
                values = G[at : at + tile, HD:] if at < n_far else VL[at - n_far : at - n_far + tile]
                result += jnp.dot(weights, values, preferred_element_type=F32)
            result = result.astype(BF)
            for g in range(some // chunk):
                head = row // chunk + g
                out_v[part, head * HD : (head + 1) * HD] = result[g * chunk : (g + 1) * chunk]
        fetch(out_v.at[part], out.at[part], 3)

    def step(r, carry):
        attend(r)

        pl.when(r == 0)(parts[2].third)
        pl.when(r == 1)(parts[3].third)

        @pl.when(r < n_chunks - 1)
        def _():
            take(H.at[0, pl.ds(0, chunk + 2 * parts[3].cut)], k_recv.at[r + 1, 6])
            project(r + 1)

        return carry

    lax.fori_loop(0, n_chunks, step, 0)

    take(out_v, l_sem.at[3])
    pl.when(has_extra)(extra.sent)
    for part in parts:
        part.sent()
    take(all_shares, a_sem.at[2])
    take(G.at[0:slots], c_send.at[0])
    take(G.at[0 : 14 * slots], c_send.at[1])
    take(G.at[0:half_far], c_send.at[2])

    @pl.when(ctx == 0)
    def _():
        take(H.at[0, pl.ds(0, (n_ctx - 1) * share)], a_sem.at[0])


def per_device(n_kv, n_ctx, hidden, w_query, w_key, w_value, keep_rows, keep_count):
    rows, depth = hidden.shape
    keep = keep_rows.shape[0]
    groups = w_query.shape[1] // HD
    nz = n_ctx // 4
    share = rows // n_ctx
    slots = keep + share
    freq = 500000.0 ** (-(np.arange(HD // 2, dtype=np.float64) * 2.0 / HD))
    freq = jnp.asarray(np.broadcast_to(np.concatenate([freq, freq]), (8, HD)), F32)
    any_spec = pl.BlockSpec(memory_space=pl.ANY)
    smem = pl.BlockSpec(memory_space=pltpu.SMEM)
    n_far = n_ctx * slots
    return pl.pallas_call(
        functools.partial(kernel, (rows, keep, share, groups, n_ctx, nz)),
        out_shape=jax.ShapeDtypeStruct((rows, groups * HD), BF),
        in_specs=[any_spec] * 4 + [smem, smem, any_spec],
        out_specs=any_spec,
        scratch_shapes=[
            pltpu.VMEM((n_kv, rows, depth), BF),
            pltpu.VMEM((n_kv, slots, depth), BF),
            pltpu.VMEM((n_kv * depth, (groups + 2) * HD), BF),
            pltpu.VMEM((n_far, 2 * HD), BF),
            pltpu.VMEM((n_far, HD), BF),
            pltpu.VMEM((rows, HD), BF),
            pltpu.VMEM((rows, HD), BF),
            pltpu.VMEM((rows * groups, HD), BF),
            pltpu.VMEM((groups * 128, n_far + rows), F32),
            pltpu.VMEM((rows, HD), F32),
            pltpu.VMEM((rows, HD), F32),
            pltpu.VMEM((8, HD), F32),
            pltpu.VMEM((rows, groups * HD), BF),
            pltpu.SemaphoreType.DMA((rows // 128 + 1,)),
            pltpu.SemaphoreType.DMA((rows // 128 + 1, 7)),
            pltpu.SemaphoreType.DMA((4,)),
            pltpu.SemaphoreType.DMA((3,)),
            pltpu.SemaphoreType.DMA((11,)),
            pltpu.SemaphoreType.DMA((4,)),
        ],
        compiler_params=pltpu.CompilerParams(
            collective_id=0, has_side_effects=True, vmem_limit_bytes=58 << 20
        ),
        name="prefill",
    )(hidden, w_query, w_key, w_value, keep_rows, keep_count, freq)


def solution(mesh):
    in_specs = (P("ctx", "kv"), P(None, "kv"), P(None, "kv"), P(None, "kv"), P("ctx"), P())
    out_specs = P("ctx", "kv")
    step = functools.partial(per_device, mesh.shape["kv"], mesh.shape["ctx"])
    return jax.shard_map(step, mesh=mesh, in_specs=in_specs, out_specs=out_specs, check_vma=False)
```

```python
import functools
import math

import jax
import jax.numpy as jnp
import numpy as np
from jax import lax
from jax.experimental import pallas as pl
from jax.experimental.pallas import tpu as pltpu
from jax.sharding import PartitionSpec as P

HD = 128
MESH = pl.DeviceIdType.MESH
BF = jnp.bfloat16
F32 = jnp.float32
SCALE = math.log2(math.e) / math.sqrt(HD)


def up16(n):
    return (n + 15) // 16 * 16


def send(part, dst, device, send_sem, recv_sem):
    copy = pltpu.make_async_remote_copy(
        src_ref=part, dst_ref=dst, send_sem=send_sem, recv_sem=recv_sem, device_id=device, device_id_type=MESH
    )
    copy.start()
    return copy


def take(like, sem):
    pltpu.make_async_copy(like, like, sem).wait()


class Gather:
    def __init__(self, sems, index, like, buf, base, rows, cut, kv_at, source):
        self.flip = index % 2
        self.buf, self.base, self.rows, self.cut, self.at, self.source = buf, base, rows, cut, kv_at, source
        self.send_sem, self.recv = sems[0].at[index], [sems[1].at[index, i] for i in range(7)]
        self.like = like

    def part(self, dx, dy, lo, hi):
        return self.buf.at[self.at(dx, dy), pl.ds(self.base + lo, hi - lo)]

    def fwd(self, part, dx, dy, sem):
        return send(part, part, {"kv": self.at(dx, dy)}, self.send_sem, self.recv[sem])

    def own(self, ways=(0, 1, 2)):
        dst = self.part(0, 0, 0, self.rows)
        for i in ways:
            device = {"kv": self.at(*((1, 0), (3, 0), (0, 1))[i])}
            send(self.source, dst, device, self.send_sem, self.recv[i])

    def took(self, rows, sem):
        take(self.like.at[0, pl.ds(0, rows)], self.recv[sem])

    def second(self):
        n, cut, half = self.rows, self.cut, up16(self.rows // 2)
        self.took(n, 2)
        part = self.part(0, 1, cut, n)
        self.fwd(part, 1, 0, 3)
        self.fwd(part, 3, 0, 4)
        self.took(n, 0)
        self.fwd(self.part(3, 0, 0, half), 1, 0, 5)
        self.fwd(self.part(3, 0, 0, cut), 0, 1, 6)
        self.took(n, 1)
        self.fwd(self.part(1, 0, half, n), 3, 0, 5)
        self.fwd(self.part(1, 0, 0, cut), 0, 1, 6)

    def third(self):
        n, cut = self.rows, self.cut
        mid = cut + up16((n - cut) // 2)
        if self.flip:
            mid = n + cut - mid
        self.took(n - cut, 3)
        self.fwd(self.part(3, 1, cut, mid), 1, 0, 6)
        self.took(n - cut, 4)
        self.fwd(self.part(1, 1, mid, n), 3, 0, 6)
        self.took(n, 5)
        self.fwd(self.part(2, 0, 0, cut), 0, 1, 6)

    def finish(self):
        self.took(self.rows + 2 * self.cut, 6)

    def sent(self):
        take(self.like.at[0:7, pl.ds(0, self.rows)], self.send_sem)


def rope(field, cosine, sine):
    return field * cosine + pltpu.roll(field, HD // 2, 1) * sine


def tables(places, freq, sign):
    angles = places * freq
    return jnp.cos(angles), jnp.sin(angles) * sign


def lane_fold(op, s, total):
    for k in range(0, s.shape[1], HD):
        total = op(total, s[:, k : k + HD])
    return total


def kernel(
    sizes,
    hidden, w_query, w_key, w_value, keep_rows, keep_count, freq,
    out,
    H, RH, W, G, bias, KL, VL, Q, S, cos_t, sin_t, freq_v, out_v,
    k_send, k_recv, a_sem, c_send, c_recv, l_sem,
):
    rows, keep, share, groups, n_ctx, nz = sizes
    chunk = 128
    n_chunks = rows // chunk
    slots = keep + share
    depth = hidden.shape[1]
    n_src = H.shape[0]
    many = groups * chunk
    n_far = n_ctx * slots
    kv = lax.axis_index("kv")
    ctx = lax.axis_index("ctx")
    kx, ky = kv // 2, kv % 2
    yh, z, core = ctx // (2 * nz), (ctx // 2) % nz, ctx % 2

    def kv_at(dx, dy):
        return ((kx + dx) % 4) * 2 + (ky + dy) % 2

    def ctx_at(dy, dz, dc):
        return ((yh + dy) % 2) * (2 * nz) + ((z + dz) % nz) * 2 + (core + dc) % 2

    def fetch(src, dst, sem):
        copy = pltpu.make_async_copy(src, dst, l_sem.at[sem])
        copy.start()
        return copy

    barrier = pltpu.get_barrier_semaphore()
    kv_near = [(dx, dy) for dx in range(4) for dy in range(2) if dx or dy]
    ctx_near = ((1, 0, 0), (0, 1, 0), (0, nz - 1, 0), (0, 2, 0), (0, nz - 2, 0), (0, 0, 1))

    @pl.when(ctx != 0)
    def _():
        pl.semaphore_signal(barrier, inc=1, device_id={"ctx": 0}, device_id_type=MESH)

    for step in ctx_near:
        pl.semaphore_signal(barrier, inc=1, device_id={"ctx": ctx_at(*step)}, device_id_type=MESH)
    for step in kv_near:
        pl.semaphore_signal(barrier, inc=1, device_id={"kv": kv_at(*step)}, device_id_type=MESH)

    own_here = fetch(hidden, H.at[kv], 0)
    got_freq = fetch(freq, freq_v, 1)
    fetch(w_key, W.at[:, pl.ds(groups * HD, HD)], 2)
    fetch(w_value, W.at[:, pl.ds((groups + 1) * HD, HD)], 2)
    fetch(w_query, W.at[:, pl.ds(0, groups * HD)], 2)

    place_of = lax.broadcasted_iota(jnp.int32, (keep, HD), 0)
    picked = jnp.zeros((keep, HD), jnp.int32)
    for j in range(keep):
        picked = jnp.where(place_of == j, keep_rows[j], picked)
    lanes = lax.broadcasted_iota(jnp.int32, (keep, HD), 1)
    one_hot = jnp.concatenate(
        [(lanes + k * HD == picked).astype(F32).astype(BF) for k in range(rows // HD)], axis=1
    )
    own_here.wait()

    has_extra = ctx != 0

    @pl.when(has_extra)
    def _():
        RH[kv, 0:keep] = jnp.dot(one_hot, H[kv], preferred_element_type=F32).astype(BF)

    @pl.when(ctx == 0)
    def _():
        RH[:, 0:keep] = jnp.zeros((n_src, keep, depth), BF)


    near = len(kv_near) + len(ctx_near)
    pl.semaphore_wait(barrier, jnp.where(ctx == 0, near + n_ctx - 1, near))

    anchor_slot = RH.at[kv, pl.ds(keep, share)]

    def anchor_copy(c):
        return pltpu.make_async_remote_copy(
            src_ref=hidden.at[pl.ds(c * share, share)],
            dst_ref=anchor_slot,
            send_sem=a_sem.at[0],
            recv_sem=a_sem.at[1],
            device_id={"ctx": c},
            device_id_type=MESH,
        )

    @pl.when(ctx == 0)
    def _():
        def body(c, carry):
            anchor_copy(c).start()
            return carry

        lax.fori_loop(1, n_ctx, body, 0)
        mine = pltpu.make_async_copy(hidden.at[pl.ds(0, share)], anchor_slot, a_sem.at[1])
        mine.start()

    sems = (k_send, k_recv)
    extra = Gather(sems, n_chunks, H, RH, 0, keep, keep // 2, kv_at, RH.at[kv, pl.ds(0, keep)])
    parts = [
        Gather(sems, r, H, H, r * chunk, chunk, (48 if r else 64), kv_at, hidden.at[pl.ds(r * chunk, chunk)])
        for r in range(n_chunks)
    ]
    pl.when(has_extra)(extra.own)

    KL[...] = jnp.zeros_like(KL)
    VL[...] = jnp.zeros_like(VL)
    row_of = lax.broadcasted_iota(jnp.int32, (slots, HD), 0)
    first_lane = lax.broadcasted_iota(jnp.int32, (slots, HD), 1) == 0

    def mark(i, carry):
        c = (i % 2) * (2 * nz) + ((i // 2) % nz) * 2 + i // (2 * nz)
        limit = jnp.where((c >= 1) & (c < ctx), keep_count[c], 0)
        anchors = jnp.where(ctx >= 1, slots, 0)
        live = row_of < jnp.where(row_of < keep, limit, anchors)
        at = pl.ds(pl.multiple_of(i * slots, 16), slots)
        bias[at, :] = jnp.where(first_lane & jnp.logical_not(live), -1e30, 0.0).astype(BF)
        return carry

    lax.fori_loop(0, n_ctx, mark, 0)

    pl.when(has_extra)(extra.second)
    parts[0].own()

    got_freq.wait()
    freq_row = freq_v[0:1, :]
    lane = lax.broadcasted_iota(jnp.int32, (1, HD), 1)
    sign = jnp.where(lane < HD // 2, -1.0, 1.0)

    def table_of(i, carry):
        at = pl.ds(pl.multiple_of(i * 64, 64), 64)
        places = (ctx * rows + i * 64 + lax.broadcasted_iota(jnp.int32, (64, HD), 0)).astype(F32)
        cos_t[at, :], sin_t[at, :] = tables(places, freq_row, sign)
        return carry

    lax.fori_loop(0, rows // 64, table_of, 0)
    extra_places = jnp.concatenate(
        [
            (ctx * rows + picked).astype(F32),
            (ctx * share + lax.broadcasted_iota(jnp.int32, (share, HD), 0)).astype(F32),
        ],
        axis=0,
    )
    extra_cos, extra_sin = tables(extra_places, freq_row, sign)

    pl.when(has_extra)(extra.third)
    anchor_copy(0).wait_recv()
    for step in kv_near:
        send(anchor_slot, anchor_slot, {"kv": kv_at(*step)}, a_sem.at[2], a_sem.at[3])
    parts[1].own((0, 1))
    parts[0].second()
    pl.when(has_extra)(extra.finish)
    all_shares = H.at[0:7, pl.ds(0, share)]
    take(all_shares, a_sem.at[3])
    def block_at(at_z, at_y):
        return pl.ds(pl.multiple_of(((core * nz + at_z) * 2 + at_y) * slots, slots), slots)

    take(W, l_sem.at[2])
    kv_cols = slice(groups * HD, (groups + 2) * HD)
    raw = jnp.zeros((slots, 2 * HD), F32)
    for s in range(n_src):
        raw += jnp.dot(RH[s], W[s * depth : (s + 1) * depth, kv_cols], preferred_element_type=F32)
    own_block = block_at(z, yh)
    G[own_block, 0:HD] = rope(raw[:, :HD], extra_cos, extra_sin).astype(BF)
    G[own_block, HD:] = raw[:, HD:].astype(BF)

    def hop(part, step, send_sem, recv_sem):
        send(part, part, {"ctx": ctx_at(*step)}, c_send.at[send_sem], c_recv.at[recv_sem])

    def at_z(dz):
        return G.at[pl.ds(pl.multiple_of((core * nz + (z + dz) % nz) * 2 * slots, 2 * slots), 2 * slots)]

    def to_core(part):
        hop(part, (0, 0, 1), 2, 8)

    near_z = ((2, 1, 9), (nz - 2, 2, 10), (1, 3, 3), (nz - 1, 4, 4))
    block = G.at[own_block]
    hop(block, (1, 0, 0), 0, 0)
    for dz, sem, _ in near_z:
        hop(block, (0, dz, 0), 1, sem)
    parts[1].own((2,))

    def project(r):
        part = pl.ds(pl.multiple_of(r * chunk, chunk), chunk)
        raw = jnp.zeros((chunk, (groups + 2) * HD), F32)
        for s in range(n_src):
            raw += jnp.dot(H[s, part], W[s * depth : (s + 1) * depth], preferred_element_type=F32)
        cosine, sine = cos_t[part, :], sin_t[part, :]
        for g in range(groups):
            at = pl.ds(pl.multiple_of(r * many + g * chunk, chunk), chunk)
            Q[at, :] = rope(raw[:, g * HD : (g + 1) * HD], cosine, sine).astype(BF)
        KL[part, :] = rope(raw[:, groups * HD : (groups + 1) * HD], cosine, sine).astype(BF)
        VL[part, :] = raw[:, (groups + 1) * HD :].astype(BF)

    parts[0].third()
    take(block, c_recv.at[0])
    block = G.at[block_at(z, 1 - yh)]
    for dz, _, sem in near_z:
        hop(block, (0, dz, 0), 1, sem)
    to_core(at_z(0))

    def onward(which):
        at_y = (yh, 1 - yh)[which]
        for i, (dz, *sems_z) in enumerate(near_z[:2]):
            got = G.at[block_at((z + nz - dz) % nz, at_y)]
            take(got, c_recv.at[sems_z[which]])
            hop(got, (0, (1, nz - 1)[i], 0), 1, 5 + i)
            if i == which:
                hop(got, (0, dz, 0), 1, 7)

    onward(0)
    parts[2].own()
    parts[1].second()
    parts[3].own()
    onward(1)
    for dz, _, sem in near_z:
        got = at_z(nz - dz)
        if dz in (1, nz - 1):
            take(got, c_recv.at[sem])
        to_core(got)
    parts[0].finish()
    project(0)
    for i, dz in enumerate((3, nz - 3)):
        got = at_z(nz - dz)
        take(got, c_recv.at[5 + i])
        to_core(got)
    got = at_z(nz // 2)
    take(got, c_recv.at[7])
    to_core(got)
    parts[1].third()
    parts[2].second()
    parts[3].second()
    half_far = n_far // 2
    take(G.at[0:half_far], c_recv.at[8])

    contract = (((1,), (1,)), ((), ()))
    in_chunk = lax.broadcasted_iota(jnp.int32, (many, rows), 0) % chunk
    key_place = lax.broadcasted_iota(jnp.int32, (many, rows), 1)
    adds_bias = (lax.broadcasted_iota(jnp.int32, (many, HD), 1) == 0).astype(F32).astype(BF)
    tile = 512
    tiles = range(0, n_far, tile)
    some = many // 2

    def attend(r):
        q = Q[pl.ds(pl.multiple_of(r * many, many), many), :]
        q_wide = jnp.concatenate([q, adds_bias], axis=1)
        s = lax.dot_general(q, KL[...], contract, preferred_element_type=F32)
        s = jnp.where(key_place <= in_chunk + r * chunk, s, -jnp.inf)
        S[:, n_far:] = s
        top = lane_fold(jnp.maximum, s[:, HD:], s[:, :HD])
        for at in tiles:
            keys = jnp.concatenate([G[at : at + tile, :HD], bias[at : at + tile]], axis=1)
            s = lax.dot_general(q_wide, keys, contract, preferred_element_type=F32)
            S[:, at : at + tile] = s
            top = lane_fold(jnp.maximum, s, top)
        top = jnp.max(top, axis=1, keepdims=True) * SCALE
        part = pl.ds(pl.multiple_of(r * chunk, chunk), chunk)
        for row in range(0, many, some):
            mine = slice(row, row + some)
            total = jnp.zeros((some, HD), F32)
            for at in range(0, n_far + rows, tile):
                e = jnp.exp2(S[mine, at : at + tile] * SCALE - top[mine])
                S[mine, at : at + tile] = e
                total = lane_fold(jnp.add, e, total)
            part_of = 1.0 / jnp.sum(total, axis=1, keepdims=True)
            result = jnp.zeros((some, HD), F32)
            for at in range(0, n_far + rows, tile):
                weights = (S[mine, at : at + tile] * part_of).astype(BF)
                values = G[at : at + tile, HD:] if at < n_far else VL[at - n_far : at - n_far + tile]
                result += jnp.dot(weights, values, preferred_element_type=F32)
            result = result.astype(BF)
            for g in range(some // chunk):
                head = row // chunk + g
                out_v[part, head * HD : (head + 1) * HD] = result[g * chunk : (g + 1) * chunk]
        fetch(out_v.at[part], out.at[part], 3)

    def step(r, carry):
        attend(r)

        pl.when(r == 0)(parts[2].third)
        pl.when(r == 1)(parts[3].third)

        @pl.when(r < n_chunks - 1)
        def _():
            take(H.at[0, pl.ds(0, chunk + 2 * parts[3].cut)], k_recv.at[r + 1, 6])
            project(r + 1)

        return carry

    lax.fori_loop(0, n_chunks, step, 0)

    take(out_v, l_sem.at[3])
    pl.when(has_extra)(extra.sent)
    for part in parts:
        part.sent()
    take(all_shares, a_sem.at[2])
    take(G.at[0:slots], c_send.at[0])
    take(G.at[0 : 14 * slots], c_send.at[1])
    take(G.at[0:half_far], c_send.at[2])

    @pl.when(ctx == 0)
    def _():
        take(H.at[0, pl.ds(0, (n_ctx - 1) * share)], a_sem.at[0])


def per_device(n_kv, n_ctx, hidden, w_query, w_key, w_value, keep_rows, keep_count):
    rows, depth = hidden.shape
    keep = keep_rows.shape[0]
    groups = w_query.shape[1] // HD
    nz = n_ctx // 4
    share = rows // n_ctx
    slots = keep + share
    freq = 500000.0 ** (-(np.arange(HD // 2, dtype=np.float64) * 2.0 / HD))
    freq = jnp.asarray(np.broadcast_to(np.concatenate([freq, freq]), (8, HD)), F32)
    any_spec = pl.BlockSpec(memory_space=pl.ANY)
    smem = pl.BlockSpec(memory_space=pltpu.SMEM)
    n_far = n_ctx * slots
    return pl.pallas_call(
        functools.partial(kernel, (rows, keep, share, groups, n_ctx, nz)),
        out_shape=jax.ShapeDtypeStruct((rows, groups * HD), BF),
        in_specs=[any_spec] * 4 + [smem, smem, any_spec],
        out_specs=any_spec,
        scratch_shapes=[
            pltpu.VMEM((n_kv, rows, depth), BF),
            pltpu.VMEM((n_kv, slots, depth), BF),
            pltpu.VMEM((n_kv * depth, (groups + 2) * HD), BF),
            pltpu.VMEM((n_far, 2 * HD), BF),
            pltpu.VMEM((n_far, HD), BF),
            pltpu.VMEM((rows, HD), BF),
            pltpu.VMEM((rows, HD), BF),
            pltpu.VMEM((rows * groups, HD), BF),
            pltpu.VMEM((groups * 128, n_far + rows), F32),
            pltpu.VMEM((rows, HD), F32),
            pltpu.VMEM((rows, HD), F32),
            pltpu.VMEM((8, HD), F32),
            pltpu.VMEM((rows, groups * HD), BF),
            pltpu.SemaphoreType.DMA((rows // 128 + 1,)),
            pltpu.SemaphoreType.DMA((rows // 128 + 1, 7)),
            pltpu.SemaphoreType.DMA((4,)),
            pltpu.SemaphoreType.DMA((3,)),
            pltpu.SemaphoreType.DMA((11,)),
            pltpu.SemaphoreType.DMA((4,)),
        ],
        compiler_params=pltpu.CompilerParams(
            collective_id=0, has_side_effects=True, vmem_limit_bytes=58 << 20
        ),
        name="prefill",
    )(hidden, w_query, w_key, w_value, keep_rows, keep_count, freq)


def solution(mesh):
    in_specs = (P("ctx", "kv"), P(None, "kv"), P(None, "kv"), P(None, "kv"), P("ctx"), P())
    out_specs = P("ctx", "kv")
    step = functools.partial(per_device, mesh.shape["kv"], mesh.shape["ctx"])
    return jax.shard_map(step, mesh=mesh, in_specs=in_specs, out_specs=out_specs, check_vma=False)
```
